128 devices in a mesh: bins: 8 (over y, core), cells: 16 (over z, x).
Axes of the slice: x: 4, y: 4, z: 4, core: 2. Of those that a mesh axis runs over, the one named last changes fastest.
Arguments:
- concen: bfloat16 [1024, 128, 1024], P('bins', 'cells'), may hold values from 0.049804688 to 2
- courant: float32 [2, 128, 1024], P(None, 'cells'), may hold values from -0.45 to 0.45
- saturation: float32 [128, 1024], P('cells', 'bins'), may hold values from 0.2 to 1.5
- growth: float32 [1024], replicated, may hold values from 0.05 to 0.5
- kernel: bfloat16 [8, 8, 128, 128], replicated, may hold values from 9.9658966e-05 to 0.0039978027
- redist: bfloat16 [8, 8, 128, 128], replicated, may hold values from 0.00019454956 to 0.0078125
- pair_lists: int32 [128, 64], replicated, may hold values from 0 to 63, each once within a row
- active_count: int32 [128], replicated, may hold values from 4 to 48, as said below
Outputs:
- updated: bfloat16 [1024, 128, 1024], P('bins', 'cells')
The draws below stay inside these ranges and needn't reach their ends.
Inputs may be any that keep to these rules, and one draw needn't show every extreme that they name: `pair_lists`: each row holds every pair number once. `active_count`: some tile has exactly 48 active pairs.
All inputs are finite; a program needn't handle non-finite values.
Results may differ from the reference program's by a relative error of at most 0.001.
The reference program's roundings to bfloat16 on the way (of `first`, `losses` and `middle`) count: a program that leaves them out, or rounds other values in their place, can miss the bound.
Values may be sent and summed in bfloat16 or wider, within the bound.
No kernel may reach another device: no remote copies, remote signals or barrier semaphores. Data moves between devices by JAX's collectives and lax.ppermute only.
A program may use at most 64 MiB of HBM per device.

```python
import math
import jax
import jax.numpy as jnp
from jax import lax

BINS = 1024
BLOCK = 128
RX = 8
NY = 1024
SUB = 2
NB = 8
NPAIRS = 64
MAXP = 48
MINP = 4
NX = 128
TILE_Y = 128
TILES = 128
N_BINS = 8
N_CELLS = 16


def draw_active_count(key, part):
    key = jax.random.fold_in(key, 7)
    first_key, second_key = jax.random.split(key)
    spread = MAXP - MINP
    uniform_ints = jax.random.randint(first_key, (TILES,), 0, spread + 1)
    counts = MINP + uniform_ints * uniform_ints // spread
    busiest = jax.random.randint(second_key, (), 0, TILES)
    counts = jnp.where(jnp.arange(TILES) == busiest, MAXP, counts)
    return counts.astype(jnp.int32)


def levels(stream_key, shape, shards, least, largest):
    factor_of = 1.0
    for dim, parts in shards:
        steps = jax.random.uniform(jax.random.fold_in(jax.random.fold_in(stream_key, 6), dim), (parts,), jnp.float32, least / len(shards), largest / len(shards))
        factor_of = factor_of * jnp.repeat(jnp.exp(steps), shape[dim] // parts).reshape((-1,) + (1,) * (len(shape) - 1 - dim))
    return factor_of


def setup_inputs(seed: int = 0) -> dict:
    splits = jax.random.split(jax.random.key(seed), 9)
    return {
        "concen": jnp.clip(jnp.exp(math.log(2.0) - 3.6927934 * jax.random.uniform(splits[0], (BINS, NX, NY), jnp.float32) ** levels(splits[0], (BINS, NX, NY), ((0, 8), (1, 16)), -0.2, 0.2)), 0.049804688, 2.0).astype(jnp.bfloat16),
        "courant": jnp.clip(jax.random.uniform(splits[1], (2, NX, NY), jnp.float32, -0.45, 0.45) * levels(splits[1], (2, NX, NY), ((1, 16),), -0.4, 0.0), -0.45, 0.45),
        "saturation": jnp.clip(0.2 + 1.3 * jax.random.uniform(splits[2], (NX, NY), jnp.float32) ** levels(splits[2], (NX, NY), ((0, 16), (1, 8)), -0.2, 0.2), 0.2, 1.5),
        "growth": jnp.clip(jnp.exp(jax.random.uniform(splits[3], (BINS,), jnp.float32, math.log(0.05), math.log(0.5))), 0.05, 0.5),
        "kernel": jnp.clip(jnp.exp(jax.random.uniform(splits[4], (NB, NB, BLOCK, BLOCK), jnp.float32, math.log(9.965896606445312e-05), math.log(0.0039978027))), 9.965896606445312e-05, 0.0039978027).astype(jnp.bfloat16),
        "redist": jnp.clip(jnp.exp(jax.random.uniform(splits[5], (NB, NB, BLOCK, BLOCK), jnp.float32, math.log(0.00019454956), math.log(0.0078125))), 0.00019454956, 0.0078125).astype(jnp.bfloat16),
        "pair_lists": jax.vmap(lambda own: jax.random.permutation(own, NPAIRS))(jax.random.split(splits[6], TILES)).reshape((TILES, NPAIRS)).astype(jnp.int32),
        "active_count": draw_active_count(jax.random.fold_in(splits[8], 71), 0),
    }


def advect_grid(fields, courant):
    right = jnp.roll(fields, -1, 1)
    above = jnp.roll(fields, -1, 2)
    flux_x = jnp.maximum(courant[0], 0.0) * fields + jnp.minimum(courant[0], 0.0) * right
    flux_y = jnp.maximum(courant[1], 0.0) * fields + jnp.minimum(courant[1], 0.0) * above
    return fields - flux_x + jnp.roll(flux_x, 1, 1) - flux_y + jnp.roll(flux_y, 1, 2)


def block_sum(matrices, sources, pair_row, active):
    nblocks = matrices.shape[0]

    def add_pair(index, totals):
        pair_id = pair_row[index]
        row_block = pair_id // nblocks
        col_block = pair_id % nblocks
        tile_matrix = lax.dynamic_index_in_dim(lax.dynamic_index_in_dim(matrices, row_block, 0, False), col_block, 0, False)
        source = lax.dynamic_index_in_dim(sources, col_block, 0, False)
        current = lax.dynamic_index_in_dim(totals, row_block, 0, False)
        update = current + jnp.dot(tile_matrix, source, preferred_element_type=jnp.float32)
        return lax.dynamic_update_index_in_dim(totals, update, row_block, 0)

    start = jnp.zeros((nblocks, sources.shape[1], sources.shape[2]), jnp.float32)
    return lax.fori_loop(0, active, add_pair, start)


def coagulate(concen, kernel, redist, pair_row, active):
    nblocks = kernel.shape[0]
    block_size = kernel.shape[2]
    blocks = concen.reshape(nblocks, block_size, concen.shape[1])
    collide = block_sum(kernel, blocks, pair_row, active)
    losses = blocks.astype(jnp.float32) * collide
    formed = block_sum(redist, losses.astype(jnp.bfloat16), pair_row, active)
    return (blocks.astype(jnp.float32) - losses + formed).reshape(concen.shape)


def condense(after, satur, growth):
    flux = growth[:, None] * satur[None, :] * after
    inflow = jnp.concatenate([jnp.zeros_like(flux[:1]), flux[:-1]], 0)
    return (after - flux + inflow).astype(jnp.bfloat16)


def reference(concen, courant, saturation, growth, kernel, redist, pair_lists, active_count):
    fields = concen.astype(jnp.float32)
    for substep in range(SUB):
        fields = advect_grid(fields, courant)
    first = fields.astype(jnp.bfloat16)
    tiled = first.reshape(BINS, N_CELLS, RX, N_BINS, TILE_Y)
    tiled = tiled.transpose(3, 1, 0, 2, 4).reshape(TILES, BINS, RX * TILE_Y)
    sat_tiles = saturation.reshape(N_CELLS, RX, N_BINS, TILE_Y).transpose(2, 0, 1, 3).reshape(TILES, RX * TILE_Y)

    def one_tile(tile_id):
        after = coagulate(tiled[tile_id], kernel, redist, pair_lists[tile_id], active_count[tile_id])
        return condense(after, sat_tiles[tile_id], growth)

    finished = lax.map(one_tile, jnp.arange(TILES, dtype=jnp.int32))
    middle = finished.reshape(N_BINS, N_CELLS, BINS, RX, TILE_Y).transpose(2, 1, 3, 0, 4).reshape(BINS, NX, NY)
    fields = middle.astype(jnp.float32)
    for substep in range(SUB):
        fields = advect_grid(fields, courant)
    return fields.astype(jnp.bfloat16)
```

```python
import jax
import jax.numpy as jnp
from jax import lax
from jax.experimental import pallas as pl
from jax.experimental.pallas import tpu as pltpu
from jax.sharding import PartitionSpec as P

STEP = 32
GROUP = 16
VMEM = 56 * 2**20


def shifted(value, axis, steps):
    count = lax.axis_size(axis)
    pairs = [(source, (source + steps) % count) for source in range(count)]
    return lax.ppermute(value, axis, pairs)


def params():
    return pltpu.CompilerParams(vmem_limit_bytes=VMEM)


def cost(flops, read):
    return pl.CostEstimate(flops=flops, bytes_accessed=read, transcendentals=0)


def split_rows_kernel(x_ref, low_ref, mid_ref, high_ref, scratch):
    rows, width = x_ref.shape[1], x_ref.shape[2]
    for group in range(STEP // GROUP):
        part = x_ref[pl.ds(group * GROUP, GROUP)].astype(jnp.float32)
        part = part.reshape(GROUP * rows, width)
        for tile in range(width // 128):
            scratch[tile] = part[:, tile * 128 : (tile + 1) * 128]
        for row in range(rows):
            for lane in range(0, width, 128):
                value = scratch[lane // 128, pl.ds(row, GROUP, stride=rows), :].astype(jnp.bfloat16)
                dest, index = (low_ref, row) if row < 2 else (mid_ref, row - 2) if row < 6 else (high_ref, row - 6)
                dest[index, pl.ds(group * GROUP, GROUP), pl.ds(lane, 128)] = value


def split_rows(concen):
    bins, rows, width = concen.shape
    out = lambda n: jax.ShapeDtypeStruct((n, bins, width), concen.dtype)
    spec = lambda n: pl.BlockSpec((n, STEP, width), lambda i: (0, i, 0))
    return pl.pallas_call(
        split_rows_kernel,
        grid=(bins // STEP,),
        in_specs=[pl.BlockSpec((STEP, rows, width), lambda i: (i, 0, 0))],
        out_specs=[spec(2), spec(4), spec(2)],
        out_shape=[out(2), out(4), out(2)],
        scratch_shapes=[pltpu.VMEM((width // 128, GROUP * rows, 128), jnp.float32)],
        compiler_params=params(),
        cost_estimate=cost(0, 4 * bins * rows * width),
        name="split_rows",
    )(concen)


def fill_coefs(coef, rates, first_row, last_row):
    for row in range(first_row, last_row + 1):
        face_x, face_y = rates(0, row), rates(1, row)
        under = rates(0, row - 1)
        left = pltpu.roll(jnp.broadcast_to(face_y, (8, face_y.shape[1])), 1, 1)
        face_x, face_y, under = (jnp.broadcast_to(v, left.shape) for v in (face_x, face_y, under))
        out_y, in_y = jnp.maximum(face_y, 0.0), jnp.minimum(left, 0.0)
        own = 1.0 - jnp.maximum(face_x, 0.0) + jnp.minimum(under, 0.0) - out_y + in_y
        base = 5 * (row - first_row)
        coef[base] = own
        coef[base + 1] = -jnp.minimum(face_x, 0.0)
        coef[base + 2] = jnp.maximum(under, 0.0)
        coef[base + 3] = -jnp.minimum(face_y, 0.0)
        coef[base + 4] = jnp.maximum(left, 0.0)


def substep(coef, base, before, value, after):
    width = value.shape[-1]
    total = coef[base][None] * value + coef[base + 1][None] * after + coef[base + 2][None] * before
    total += coef[base + 3][None] * pltpu.roll(value, width - 1, 2)
    return total + coef[base + 4][None] * pltpu.roll(value, 1, 2)


def two_substeps(coef, first_row, load, rows, store):
    start, stop = rows[0], rows[-1]
    once = {}
    raw = {row: load(row) for row in (start - 2, start - 1)}
    for row in range(start - 1, stop + 2):
        raw[row + 1] = load(row + 1)
        once[row] = substep(coef, 5 * (row - first_row), raw[row - 1], raw[row], raw[row + 1])
        if row - 1 >= start:
            mid = row - 1
            store(mid, substep(coef, 5 * (mid - first_row), once[mid - 1], once[mid], once[mid + 1]))


def as_groups(value):
    return value.astype(jnp.float32).reshape(GROUP // 8, 8, value.shape[-1])


def inner_kernel(rate_ref, low_ref, mid_ref, high_ref, out_ref, coef):
    width = low_ref.shape[2]

    @pl.when(pl.program_id(0) == 0)
    def _():
        fill_coefs(coef, lambda k, row: rate_ref[k, row : row + 1, :], 1, 6)

    def group_step(group, carry):
        at = pl.ds(pl.multiple_of(group * GROUP, GROUP), GROUP)

        def load(row):
            ref, index = (low_ref, row) if row < 2 else (mid_ref, row - 2) if row < 6 else (high_ref, row - 6)
            return as_groups(ref[index, at, :])

        def store(row, value):
            value = value.reshape(GROUP, width).astype(jnp.bfloat16)
            for tile in range(width // 128):
                out_ref[tile, row - 2, at, :] = value[:, tile * 128 : (tile + 1) * 128]

        two_substeps(coef, 1, load, range(2, 6), store)
        return carry

    lax.fori_loop(0, STEP // GROUP, group_step, 0)


def inner_rows(courant, low, mid, high):
    _, bins, width = low.shape
    tiles = width // 128
    spec = lambda n: pl.BlockSpec((n, STEP, width), lambda i: (0, i, 0))
    return pl.pallas_call(
        inner_kernel,
        grid=(bins // STEP,),
        in_specs=[pl.BlockSpec(courant.shape, lambda i: (0, 0, 0)), spec(2), spec(4), spec(2)],
        out_specs=pl.BlockSpec((tiles, 4, STEP, 128), lambda i: (0, 0, i, 0)),
        out_shape=jax.ShapeDtypeStruct((tiles, 4, bins, 128), low.dtype),
        scratch_shapes=[pltpu.VMEM((30, 8, width), jnp.float32)],
        compiler_params=params(),
        cost_estimate=cost(10 * 12 * bins * width, 24 * bins * width),
        name="inner_rows",
    )(courant, low, mid, high)


def all_rates(below_ref, rate_ref, above_ref):
    def rates(k, row):
        if row < 0:
            return below_ref[k, row + 2 : row + 3, :]
        if row > 7:
            return above_ref[k, row - 8 : row - 7, :]
        return rate_ref[k, row : row + 1, :]

    return rates


def outer_kernel(below_ref, rate_ref, above_ref, under_ref, low_ref, mid_ref, high_ref, over_ref, out_ref, coef):
    width = low_ref.shape[2]

    @pl.when(pl.program_id(0) == 0)
    def _():
        fill_coefs(coef, all_rates(below_ref, rate_ref, above_ref), -1, 8)

    def group_step(group, carry):
        at = pl.ds(pl.multiple_of(group * GROUP, GROUP), GROUP)

        def load(row):
            for ref, start, stop in ((under_ref, -2, 0), (low_ref, 0, 2), (mid_ref, 2, 6), (high_ref, 6, 8), (over_ref, 8, 10)):
                if start <= row < stop:
                    return as_groups(ref[row - start, at, :])

        def store(row, value):
            value = value.reshape(GROUP, width).astype(jnp.bfloat16)
            for tile in range(width // 128):
                out_ref[tile, row if row < 2 else row - 4, at, :] = value[:, tile * 128 : (tile + 1) * 128]

        two_substeps(coef, -1, load, range(0, 2), store)
        two_substeps(coef, -1, load, range(6, 8), store)
        return carry

    lax.fori_loop(0, STEP // GROUP, group_step, 0)


def outer_rows(below, courant, above, under, low, mid, high, over):
    _, bins, width = low.shape
    tiles = width // 128
    spec = lambda n: pl.BlockSpec((n, STEP, width), lambda i: (0, i, 0))
    whole = lambda a: pl.BlockSpec(a.shape, lambda i: (0, 0, 0))
    return pl.pallas_call(
        outer_kernel,
        grid=(bins // STEP,),
        in_specs=[whole(below), whole(courant), whole(above), spec(2), spec(2), spec(4), spec(2), spec(2)],
        out_specs=pl.BlockSpec((tiles, 4, STEP, 128), lambda i: (0, 0, i, 0)),
        out_shape=jax.ShapeDtypeStruct((tiles, 4, bins, 128), low.dtype),
        scratch_shapes=[pltpu.VMEM((50, 8, width), jnp.float32)],
        compiler_params=params(),
        cost_estimate=cost(12 * 12 * bins * width, 32 * bins * width),
        name="outer_rows",
    )(below, courant, above, under, low, mid, high, over)


def final_kernel(below_ref, rate_ref, above_ref, under_ref, outer_ref, inner_ref, over_ref, out_ref, coef, scratch):
    tiles = inner_ref.shape[0]
    rows, width = out_ref.shape[1], out_ref.shape[2]

    @pl.when(pl.program_id(0) == 0)
    def _():
        fill_coefs(coef, all_rates(below_ref, rate_ref, above_ref), -1, 8)

    for group in range(STEP // GROUP):
        at = pl.ds(group * GROUP, GROUP)

        def load(row):
            for ref, start, stop, shift in (
                (under_ref, -2, 0, 2),
                (outer_ref, 0, 2, 0),
                (inner_ref, 2, 6, -2),
                (outer_ref, 6, 8, -4),
                (over_ref, 8, 10, -8),
            ):
                if start <= row < stop:
                    return as_groups(jnp.concatenate([ref[tile, row + shift, at, :] for tile in range(tiles)], 1))

        def store(row, value):
            value = value.reshape(GROUP, width)
            for lane in range(0, width, 128):
                scratch[lane // 128, pl.ds(row, GROUP, stride=rows), :] = value[:, lane : lane + 128]

        two_substeps(coef, -1, load, range(0, 8), store)
        part = jnp.concatenate([scratch[tile] for tile in range(tiles)], 1)
        out_ref[at] = part.reshape(GROUP, rows, width).astype(out_ref.dtype)


def final_rows(below, courant, above, under, outer, inner, over):
    tiles, _, bins, lanes = inner.shape
    rows, width = courant.shape[1], tiles * lanes
    spec = lambda n: pl.BlockSpec((tiles, n, STEP, lanes), lambda i: (0, 0, i, 0))
    whole = lambda a: pl.BlockSpec(a.shape, lambda i: (0, 0, 0))
    return pl.pallas_call(
        final_kernel,
        grid=(bins // STEP,),
        in_specs=[whole(below), whole(courant), whole(above), spec(2), spec(4), spec(4), spec(2)],
        out_specs=pl.BlockSpec((STEP, rows, width), lambda i: (i, 0, 0)),
        out_shape=jax.ShapeDtypeStruct((bins, rows, width), inner.dtype),
        scratch_shapes=[
            pltpu.VMEM((50, 8, width), jnp.float32),
            pltpu.VMEM((tiles, GROUP * rows, lanes), jnp.float32),
        ],
        compiler_params=params(),
        cost_estimate=cost(18 * 12 * bins * width, 40 * bins * width),
        name="final_rows",
    )(below, courant, above, under, outer, inner, over)


def coagulate_kernel(pair_ref, count_ref, x_ref, satur_ref, growth_ref, kernel_ref, redist_ref, out_ref, flags, matrix, losses, kept):
    nblocks, rows, size, lanes = x_ref.shape
    bins, cells = nblocks * size, rows * lanes

    def clear(index, carry):
        flags[index] = 0
        return carry

    lax.fori_loop(0, nblocks * nblocks, clear, 0)

    def mark(index, carry):
        flags[pair_ref[index]] = 1
        return carry

    lax.fori_loop(0, count_ref[0], mark, 0)

    def select(source, row):
        for col in range(nblocks):
            live = flags[row * nblocks + col] > 0
            block = source[row, col]
            matrix[:, col * size : (col + 1) * size] = jnp.where(live, block, jnp.zeros_like(block))
        return matrix[...]

    def part(row):
        return jnp.concatenate([x_ref[row, r] for r in range(rows)], 1)

    field = jnp.concatenate([part(row) for row in range(nblocks)], 0)
    for row in range(nblocks):
        collide = jnp.dot(select(kernel_ref, row), field, preferred_element_type=jnp.float32)
        own = part(row).astype(jnp.float32)
        loss = own * collide
        losses[row * size : (row + 1) * size, :] = loss.astype(jnp.bfloat16)
        kept[row * size : (row + 1) * size, :] = own - loss
    satur = jnp.concatenate([satur_ref[r : r + 1, :] for r in range(rows)], 1)
    last = jnp.zeros((1, cells), jnp.float32)
    for row in range(nblocks):
        formed = jnp.dot(select(redist_ref, row), losses[...], preferred_element_type=jnp.float32)
        after = kept[row * size : (row + 1) * size, :] + formed
        growth = jnp.concatenate([growth_ref[row * size : (row + 1) * size, :]] * rows, 1)
        flux = growth * satur * after
        inflow = pltpu.roll(flux, 1, 0)
        at_first = lax.broadcasted_iota(jnp.int32, flux.shape, 0) == 0
        inflow = jnp.where(at_first, last, inflow)
        last = flux[size - 1 : size, :]
        middle = (after - flux + inflow).astype(out_ref.dtype)
        for r in range(rows):
            out_ref[row, r] = middle[:, r * lanes : (r + 1) * lanes]


def coagulate(pair_row, active, x, satur, growth, kernel, redist):
    nblocks, rows, size, lanes = x.shape
    bins, cells = nblocks * size, rows * lanes
    vmem = pl.BlockSpec(memory_space=pltpu.VMEM)
    smem = pl.BlockSpec(memory_space=pltpu.SMEM)
    return pl.pallas_call(
        coagulate_kernel,
        in_specs=[smem, smem, vmem, vmem, vmem, vmem, vmem],
        out_specs=vmem,
        out_shape=jax.ShapeDtypeStruct(x.shape, x.dtype),
        scratch_shapes=[
            pltpu.SMEM((nblocks * nblocks,), jnp.int32),
            pltpu.VMEM((size, bins), kernel.dtype),
            pltpu.VMEM((bins, cells), jnp.bfloat16),
            pltpu.VMEM((bins, cells), jnp.float32),
        ],
        compiler_params=params(),
        cost_estimate=cost(4 * bins * bins * cells, 4 * bins * cells + 4 * bins * bins),
        name="coagulate",
    )(pair_row, active, x, satur, growth, kernel, redist)


def exchange(value):
    return lax.all_to_all(value, "bins", split_axis=0, concat_axis=0, tiled=True)


def shards(concen, courant, saturation, growth, kernel, redist, pair_lists, active_count):
    below = shifted(courant[:, -2:], "cells", 1)
    above = shifted(courant[:, :1], "cells", -1)
    low, mid, high = split_rows(concen)
    under, over = shifted(high, "cells", 1), shifted(low, "cells", -1)
    inner = exchange(inner_rows(courant, low, mid, high))
    outer = exchange(outer_rows(below, courant, above, under, low, mid, high, over))

    tile_id = lax.axis_index("bins") * lax.axis_size("cells") + lax.axis_index("cells")
    pair_row = lax.dynamic_index_in_dim(pair_lists, tile_id, 0, False)
    active = lax.dynamic_slice_in_dim(active_count, tile_id, 1)
    satur_inner = saturation[2:6]
    satur_outer = jnp.concatenate([saturation[:2], saturation[6:]], 0)
    growth_wide = jnp.broadcast_to(growth[:, None], (growth.shape[0], 128))
    inner = coagulate(pair_row, active, inner, satur_inner, growth_wide, kernel, redist)
    outer = coagulate(pair_row, active, outer, satur_outer, growth_wide, kernel, redist)

    outer = exchange(outer)
    inner = exchange(inner)
    under, over = shifted(outer[:, 2:], "cells", 1), shifted(outer[:, :2], "cells", -1)
    return final_rows(below, courant, above, under, outer, inner, over)


def solution(mesh):
    return jax.shard_map(
        shards,
        mesh=mesh,
        in_specs=(
            P("bins", "cells", None),
            P(None, "cells", None),
            P("cells", "bins"),
            P(),
            P(),
            P(),
            P(),
            P(),
        ),
        out_specs=P("bins", "cells", None),
        check_vma=False,
    )
```

```python
import functools

import jax
import jax.numpy as jnp
from jax import lax
from jax.experimental import pallas as pl
from jax.experimental.pallas import tpu as pltpu
from jax.sharding import PartitionSpec as P

STEP = 32
CHIPS = 4
ROWS = 8
PACK = 16
MIB = 2**20
SHRINK = 64


def shifted(value, axis, steps):
    count = lax.axis_size(axis)
    pairs = [(source, (source + steps) % count) for source in range(count)]
    return lax.ppermute(value, axis, pairs)


def swapped(value):
    return lax.ppermute(value, "bins", [(i, i ^ 1) for i in range(2 * CHIPS)])


def tied(value, *others):
    return lax.optimization_barrier((value, *others))[0]


def in_hbm(value):
    return pltpu.with_memory_space_constraint(value, pltpu.HBM)


def call(body, name, place, operands, outs, scratch, mib, flops, smem=0, far=()):
    vmem_spec = pl.BlockSpec(memory_space=pltpu.VMEM)
    smem_spec = pl.BlockSpec(memory_space=pltpu.SMEM)
    specs = [smem_spec] * (1 + smem) + [vmem_spec] * (len(operands) - smem)
    operands = list(operands)
    for index in far:
        specs[1 + index] = pl.BlockSpec(memory_space=pl.ANY)
        operands[index] = in_hbm(operands[index])
    moved = sum(a.size * a.dtype.itemsize for a in (*operands, *outs))
    return pl.pallas_call(
        body,
        in_specs=specs,
        out_specs=[vmem_spec] * len(outs),
        out_shape=outs,
        scratch_shapes=scratch,
        compiler_params=pltpu.CompilerParams(vmem_limit_bytes=mib * MIB),
        cost_estimate=pl.CostEstimate(flops=flops // SHRINK, bytes_accessed=moved // SHRINK, transcendentals=0),
        name=name,
    )(place, *operands)


def steps(bins, body):
    def step(index, carry):
        body(pl.multiple_of(index * STEP, STEP))
        return carry

    lax.fori_loop(0, bins // STEP, step, 0)


def struct(shape, dtype):
    return jax.ShapeDtypeStruct(shape, dtype)


def rows_first(picked):
    shape = (len(picked) * STEP, STEP * ROWS)
    out = lax.broadcasted_iota(jnp.int32, shape, 0)
    inp = lax.broadcasted_iota(jnp.int32, shape, 1)
    slot, bin_of = out // STEP, out % STEP
    row = slot
    for index, value in enumerate(picked):
        row = jnp.where(slot == index, value, row)
    return jnp.where(inp == bin_of * ROWS + row, 1.0, 0.0).astype(jnp.bfloat16)


def bins_first():
    shape = (STEP * ROWS, ROWS * STEP)
    out = lax.broadcasted_iota(jnp.int32, shape, 0)
    inp = lax.broadcasted_iota(jnp.int32, shape, 1)
    return jnp.where(inp == (out % ROWS) * STEP + out // ROWS, 1.0, 0.0).astype(jnp.bfloat16)


def thirds(value):
    high = value.astype(jnp.bfloat16)
    rest = value - high.astype(jnp.float32)
    mid = rest.astype(jnp.bfloat16)
    low = (rest - mid.astype(jnp.float32)).astype(jnp.bfloat16)
    return [v.astype(jnp.float32) for v in (high, mid, low)]


def packed(rows):
    parts = [part for row in rows for part in thirds(row)]
    parts.append(jnp.zeros((PACK - len(parts), rows[0].shape[1]), jnp.float32))
    return jnp.concatenate(parts, 0).astype(jnp.bfloat16)


def unpacked(halo_ref, index):
    parts = halo_ref[0, halo_ref.shape[1] - PACK :, :].astype(jnp.float32)[3 * index : 3 * index + 3]
    return parts[0:1] + parts[1:2] + parts[2:3]


def edge_kernel(place_ref, source_ref, far_rate_ref, low_ref, high_ref, x_ref, rate_ref, onehot, sems, rate_sem):
    bins, width = low_ref.shape[1] - PACK, x_ref.shape[1]
    size = STEP * ROWS
    part_at = lambda index: pl.ds(index * size, size)
    copies = [
        pltpu.make_async_copy(source_ref.at[part_at(i)], x_ref.at[part_at(i)], sems.at[i]) for i in range(bins // STEP)
    ]
    rates_in = pltpu.make_async_copy(far_rate_ref, rate_ref, rate_sem)
    for copy in copies:
        copy.start()
    rates_in.start()
    onehot[...] = rows_first((0, 1, 6, 7))
    for index, copy in enumerate(copies):
        copy.wait()
        at = slice(index * STEP, (index + 1) * STEP)
        for lane in range(0, width, 256):
            lanes = slice(lane, lane + 256)
            part = jnp.dot(onehot[...], x_ref[part_at(index), lanes], preferred_element_type=jnp.float32)
            part = part.astype(jnp.bfloat16)
            for row in range(2):
                low_ref[row, at, lanes] = part[row * STEP : (row + 1) * STEP]
                high_ref[row, at, lanes] = part[(row + 2) * STEP : (row + 3) * STEP]
    rates_in.wait()
    low_ref[0, bins:, :] = packed([rate_ref[0, 0:1, :], rate_ref[1, 0:1, :]])
    high_ref[0, bins:, :] = packed([rate_ref[0, 6:7, :], rate_ref[0, 7:8, :], rate_ref[1, 7:8, :]])
    low_ref[1, bins:, :] = jnp.zeros((PACK, width), low_ref.dtype)
    high_ref[1, bins:, :] = jnp.zeros((PACK, width), low_ref.dtype)


def edge_rows(place, flat, courant):
    width, bins = flat.shape[1], flat.shape[0] // ROWS
    edge = struct((2, bins + PACK, width), flat.dtype)
    outs = [edge, edge, struct(flat.shape, flat.dtype), struct(courant.shape, courant.dtype)]
    scratch = [
        pltpu.VMEM((4 * STEP, STEP * ROWS), jnp.bfloat16),
        pltpu.SemaphoreType.DMA((bins // STEP,)),
        pltpu.SemaphoreType.DMA(()),
    ]
    return call(edge_kernel, "edge_rows", place, (flat, courant), outs, scratch, 8, 8 * STEP * flat.size, far=(0, 1))


def fill_coefs(coef, rates, first_row, last_row):
    for row in range(first_row, last_row + 1):
        face_x, face_y, under = rates(0, row), rates(1, row), rates(0, row - 1)
        face_x, face_y, under = (jnp.broadcast_to(v, (8, v.shape[1])) for v in (face_x, face_y, under))
        left = pltpu.roll(face_y, 1, 1)
        base = 5 * (row - first_row)
        own = 1.0 - jnp.maximum(face_x, 0.0) + jnp.minimum(under, 0.0)
        coef[base] = own - jnp.maximum(face_y, 0.0) + jnp.minimum(left, 0.0)
        coef[base + 1] = -jnp.minimum(face_x, 0.0)
        coef[base + 2] = jnp.maximum(under, 0.0)
        coef[base + 3] = -jnp.minimum(face_y, 0.0)
        coef[base + 4] = jnp.maximum(left, 0.0)


def substep(coef, base, before, value, after):
    width = value.shape[-1]
    total = coef[base][None] * value + coef[base + 1][None] * after + coef[base + 2][None] * before
    total += coef[base + 3][None] * pltpu.roll(value, width - 1, 2)
    return total + coef[base + 4][None] * pltpu.roll(value, 1, 2)


def two_substeps(coef, first_row, load, rows, store):
    start, stop = rows[0], rows[-1]
    once = {}
    raw = {row: load(row) for row in (start - 2, start - 1)}
    for row in range(start - 1, stop + 2):
        raw[row + 1] = load(row + 1)
        once[row] = substep(coef, 5 * (row - first_row), raw[row - 1], raw[row], raw[row + 1])
        if row - 1 >= start:
            mid = row - 1
            store(mid, substep(coef, 5 * (mid - first_row), once[mid - 1], once[mid], once[mid + 1]))


def grouped(value):
    return value.astype(jnp.float32).reshape(STEP // 8, 8, value.shape[-1])


def transpose_in(onehot, x_ref, field, start):
    width = x_ref.shape[1]
    source = pl.ds(pl.multiple_of(start * ROWS, STEP * ROWS), STEP * ROWS)
    for lane in range(0, width, 256):
        part = jnp.dot(onehot[...], x_ref[source, lane : lane + 256], preferred_element_type=jnp.float32)
        field[:, :, lane : lane + 256] = part.reshape(ROWS, STEP, 256)


def inner_kernel(place_ref, rate_ref, x_ref, out0, out1, out2, out3, coef, onehot, field, tiles):
    onehot[...] = rows_first(range(ROWS))
    fill_coefs(coef, lambda k, row: rate_ref[k, row : row + 1, :], 1, 6)

    def step(start):
        transpose_in(onehot, x_ref, field, start)
        load = lambda row: grouped(field[row])
        store = lambda row, value: send_row(place_ref, tiles, (out0, out1, out2, out3), row - 2, start, value)
        two_substeps(coef, 1, load, range(2, 6), store)

    steps(out0.shape[2], step)


def send_row(place_ref, tiles, outs, slot, start, value):
    value = value.reshape(STEP, value.shape[-1]).astype(jnp.bfloat16)
    for tile in range(2 * CHIPS):
        tiles[tile] = value[:, tile * 128 : (tile + 1) * 128]
    for away, out_ref in enumerate(outs):
        chip = lax.rem(place_ref[0] + away, CHIPS)
        for core in range(2):
            out_ref[core, slot, pl.ds(start, STEP), :] = tiles[2 * chip + core]


def first_scratch(coefs, width, dtype):
    return [
        pltpu.VMEM((5 * coefs, 8, width), jnp.float32),
        pltpu.VMEM((ROWS * STEP, ROWS * STEP), jnp.bfloat16),
        pltpu.VMEM((ROWS, STEP, width), jnp.float32),
        pltpu.VMEM((2 * CHIPS, STEP, 128), dtype),
    ]


def inner_rows(place, courant, flat):
    width, bins = flat.shape[1], flat.shape[0] // ROWS
    outs = [struct((2, 4, bins, 128), flat.dtype)] * CHIPS
    scratch = first_scratch(6, width, flat.dtype)
    return call(inner_kernel, "inner_rows", place, (courant, flat), outs, scratch, 12, 120 * bins * width)


def all_rates(below_ref, rate_ref, above_ref):
    def rates(k, row):
        if row < 0:
            return unpacked(below_ref, row + 2 + k)
        if row > 7:
            return unpacked(above_ref, k)
        return rate_ref[k, row : row + 1, :]

    return rates


def outer_kernel(place_ref, rate_ref, under_ref, x_ref, over_ref, out0, out1, out2, out3, coef, onehot, field, tiles):
    onehot[...] = rows_first(range(ROWS))
    fill_coefs(coef, all_rates(under_ref, rate_ref, over_ref), -1, 8)

    def step(start):
        transpose_in(onehot, x_ref, field, start)

        def load(row):
            if row < 0:
                return grouped(under_ref[row + 2, pl.ds(start, STEP), :])
            if row > 7:
                return grouped(over_ref[row - 8, pl.ds(start, STEP), :])
            return grouped(field[row])

        def store(row, value):
            send_row(place_ref, tiles, (out0, out1, out2, out3), row if row < 2 else row - 4, start, value)

        two_substeps(coef, -1, load, range(0, 2), store)
        two_substeps(coef, -1, load, range(6, 8), store)

    steps(out0.shape[2], step)


def outer_rows(place, courant, under, flat, over):
    width, bins = flat.shape[1], flat.shape[0] // ROWS
    outs = [struct((2, 4, bins, 128), flat.dtype)] * CHIPS
    scratch = first_scratch(10, width, flat.dtype)
    operands = (courant, under, flat, over)
    return call(outer_kernel, "outer_rows", place, operands, outs, scratch, 12, 144 * bins * width)


def arrived_kernel(place_ref, *refs):
    slots, (low_ref, high_ref) = refs[:8], refs[8:]
    core = place_ref[1]
    for away in range(CHIPS):
        for other in range(2):
            tile = 2 * lax.rem(place_ref[0] + away, CHIPS) + lax.bitwise_xor(core, other)
            lanes = pl.ds(pl.multiple_of(tile * 128, 128), 128)
            for row in range(2):
                low_ref[row, :, lanes] = slots[2 * away + other][core, row]
                high_ref[row, :, lanes] = slots[2 * away + other][core, row + 2]


def arrived_rows(place, slots):
    _, _, bins, lanes = slots[0].shape
    outs = [struct((2, bins, 2 * CHIPS * lanes), slots[0].dtype)] * 2
    return call(arrived_kernel, "arrived_rows", place, slots, outs, [], 4, 0)


def final_kernel(place_ref, first_under, rate_ref, first_over, under_ref, low_ref, high_ref, over_ref, *refs):
    slots, (out_ref, coef, onehot, tiles, back) = refs[:8], refs[8:]
    width = out_ref.shape[1]
    core = place_ref[1]
    onehot[...] = bins_first()
    fill_coefs(coef, all_rates(first_under, rate_ref, first_over), -1, 8)

    def step(start):
        at = pl.ds(start, STEP)
        for away in range(CHIPS):
            for other in range(2):
                tile = 2 * lax.rem(place_ref[0] + away, CHIPS) + lax.bitwise_xor(core, other)
                for row in range(4):
                    tiles[tile, row] = slots[2 * away + other][core, row, at, :]

        def load(row):
            for ref, first, stop in ((under_ref, -2, 0), (low_ref, 0, 2), (high_ref, 6, 8), (over_ref, 8, 10)):
                if first <= row < stop:
                    return grouped(ref[row - first, at, :])
            return grouped(jnp.concatenate([tiles[tile, row - 2] for tile in range(2 * CHIPS)], 1))

        def store(row, value):
            back[row * STEP : (row + 1) * STEP, :] = value.reshape(STEP, width).astype(jnp.bfloat16)

        two_substeps(coef, -1, load, range(ROWS), store)
        target = pl.ds(pl.multiple_of(start * ROWS, STEP * ROWS), STEP * ROWS)
        for lane in range(0, width, 256):
            part = jnp.dot(onehot[...], back[:, lane : lane + 256], preferred_element_type=jnp.float32)
            out_ref[target, lane : lane + 256] = part.astype(out_ref.dtype)

    steps(low_ref.shape[1], step)


def final_rows(place, courant, first_under, first_over, under, low, slots, high, over):
    _, bins, width = low.shape
    scratch = [
        pltpu.VMEM((50, 8, width), jnp.float32),
        pltpu.VMEM((ROWS * STEP, ROWS * STEP), jnp.bfloat16),
        pltpu.VMEM((2 * CHIPS, 4, STEP, 128), low.dtype),
        pltpu.VMEM((ROWS * STEP, width), low.dtype),
    ]
    operands = (first_under, courant, first_over, under, low, high, over, *slots)
    outs = [struct((bins * ROWS, width), low.dtype)]
    return call(final_kernel, "final_rows", place, operands, outs, scratch, 12, 216 * bins * width)[0]


def block_of(place_ref, away, other):
    return 2 * lax.rem(place_ref[0] + CHIPS - away, CHIPS) + lax.bitwise_xor(place_ref[1], other)


def matrices_kernel(place_ref, pair_ref, count_ref, growth_ref, far_kernel, far_redist, first_ref, second_ref, wide_ref, flags, kernel_ref, redist_ref, sems):
    nblocks, size = kernel_ref.shape[0], kernel_ref.shape[2]
    tile = place_ref[2]
    count = count_ref[tile]

    def copies(slot):
        row = block_of(place_ref, slot // 2, lax.rem(slot, 2))
        return [
            pltpu.make_async_copy(far.at[row], near.at[row], sems.at[side, slot])
            for side, (far, near) in enumerate(((far_kernel, kernel_ref), (far_redist, redist_ref)))
        ]

    for slot in range(nblocks):
        for copy in copies(slot):
            copy.start()
    for index in range(nblocks * nblocks):
        flags[pair_ref[tile, index]] = jnp.where(index < count, 1, 0)
    blocks = [block_of(place_ref, away, other) for away in range(CHIPS) for other in range(2)]

    def row_step(slot, carry):
        row = block_of(place_ref, slot // 2, lax.rem(slot, 2))
        at = pl.ds(pl.multiple_of(slot * size, size), size)
        for copy in copies(slot):
            copy.wait()
        for index, col in enumerate(blocks):
            live = flags[row * nblocks + col] > 0
            lanes = slice(index * size, (index + 1) * size)
            for source, dest in ((kernel_ref, first_ref), (redist_ref, second_ref)):
                block = source[row, col]
                dest[at, lanes] = jnp.where(live, block, jnp.zeros_like(block))
        wide_ref[at, :] = jnp.broadcast_to(growth_ref[pl.ds(row, 1), :], (size, size)).T
        return carry

    lax.fori_loop(0, nblocks, row_step, 0)


def matrices(place, pair_lists, active_count, growth, kernel, redist):
    nblocks, size = kernel.shape[0], kernel.shape[2]
    bins = nblocks * size
    matrix = struct((bins, bins), kernel.dtype)
    outs = [matrix, matrix, struct((bins, size), jnp.float32)]
    operands = (pair_lists, active_count, growth, kernel, redist)
    scratch = [
        pltpu.SMEM((nblocks * nblocks,), jnp.int32),
        pltpu.VMEM(kernel.shape, kernel.dtype),
        pltpu.VMEM(redist.shape, redist.dtype),
        pltpu.SemaphoreType.DMA((2, nblocks)),
    ]
    return call(matrices_kernel, "matrices", place, operands, outs, scratch, 8, 0, smem=2, far=(3, 4))


def coagulate_kernel(picked, place_ref, satur_ref, growth_ref, first_ref, second_ref, *refs):
    slots, outs, (field, losses, kept, moved) = refs[:8], refs[8:12], refs[12:]
    rows, size, lanes = slots[0].shape[1:]
    bins, cells = field.shape
    chip, core = place_ref[0], place_ref[1]
    half = bins // 2
    blocks = [block_of(place_ref, away, other) for away in range(CHIPS) for other in range(2)]
    for slot in range(2 * CHIPS):
        for r in range(rows):
            field[slot * size : (slot + 1) * size, r * lanes : (r + 1) * lanes] = slots[slot][core, r]
    for start in (0, half):
        at = slice(start, start + half)
        collide = jnp.dot(first_ref[at, :], field[...], preferred_element_type=jnp.float32)
        own = field[at, :].astype(jnp.float32)
        loss = own * collide
        losses[at, :] = loss.astype(jnp.bfloat16)
        kept[at, :] = own - loss
    satur = jnp.concatenate([satur_ref[r : r + 1, :] for r in picked], 1)
    for start in (0, half):
        at = slice(start, start + half)
        formed = jnp.dot(second_ref[at, :], losses[...], preferred_element_type=jnp.float32)
        after = kept[at, :] + formed
        growth = jnp.concatenate([growth_ref[at, :]] * rows, 1)
        flux = growth * satur * after
        kept[at, :] = after - flux
        moved[at, :] = flux
    for slot in range(2 * CHIPS):
        away, other = divmod(slot, 2)
        block = blocks[slot]
        below = lax.rem(block + 2 * CHIPS - 1, 2 * CHIPS)
        source = 2 * lax.rem(chip + CHIPS - below // 2, CHIPS) + lax.bitwise_xor(lax.rem(below, 2), core)
        last = moved[pl.ds(pl.multiple_of(source * size + size - 8, 8), 8), :][7:8, :]
        last = jnp.where(block > 0, last, jnp.zeros_like(last))
        at = slice(slot * size, (slot + 1) * size)
        inflow = pltpu.roll(moved[at, :], 1, 0)
        inflow = jnp.where(lax.broadcasted_iota(jnp.int32, inflow.shape, 0) == 0, last, inflow)
        middle = (kept[at, :] + inflow).astype(jnp.bfloat16)
        for r in range(rows):
            outs[away][lax.bitwise_xor(core, other), r] = middle[:, r * lanes : (r + 1) * lanes]


def coagulate(picked, place, satur, growth, first, second, slots):
    _, rows, size, lanes = slots[0].shape
    bins, cells = 2 * CHIPS * size, rows * lanes
    outs = [struct(slots[0].shape, slots[0].dtype)] * CHIPS
    scratch = [
        pltpu.VMEM((bins, cells), jnp.bfloat16),
        pltpu.VMEM((bins, cells), jnp.bfloat16),
        pltpu.VMEM((bins, cells), jnp.float32),
        pltpu.VMEM((bins, cells), jnp.float32),
    ]
    body = functools.partial(coagulate_kernel, picked)
    operands = (satur, growth, first, second, *slots)
    return call(body, "coagulate", place, operands, outs, scratch, 16, 4 * bins * bins * cells)


def travel(parts, direction):
    return [parts[0]] + [shifted(parts[away], "bins", 2 * direction * away) for away in range(1, CHIPS)]


def with_other_core(parts):
    slots = []
    for part in parts:
        slots += [part, swapped(part)]
    return slots


def shards(concen, courant, saturation, growth, kernel, redist, pair_lists, active_count):
    bins, rows, width = concen.shape
    device = lax.axis_index("bins")
    tile_id = device * lax.axis_size("cells") + lax.axis_index("cells")
    place = jnp.stack([device // 2, device % 2, tile_id]).astype(jnp.int32)
    flat = concen.reshape(bins * rows, width)
    low, high, flat, courant = edge_rows(place, flat, courant)
    first_under, first_over = shifted(high, "cells", 1), shifted(low, "cells", -1)
    inner = inner_rows(place, courant, tied(flat, low))
    growth = growth.reshape(2 * CHIPS, bins)
    first, second, growth = matrices(tied(place, inner[0]), pair_lists, active_count, growth, kernel, redist)
    outer = outer_rows(place, courant, first_under, tied(flat, inner[0], first), first_over)
    inner_slots = with_other_core([tied(part, outer[0]) for part in travel(inner, 1)])
    inner = coagulate((2, 3, 4, 5), place, saturation, growth, first, second, inner_slots)
    outer_slots = with_other_core([tied(part, inner[0]) for part in travel(outer, 1)])
    outer = coagulate((0, 1, 6, 7), place, saturation, growth, first, second, outer_slots)

    outer_slots = with_other_core(travel(outer, -1))
    inner_slots = with_other_core(travel([tied(part, outer[0]) for part in inner], -1))
    low, high = arrived_rows(place, outer_slots)
    under, over = shifted(high, "cells", 1), shifted(low, "cells", -1)
    out = final_rows(place, courant, first_under, first_over, under, low, inner_slots, high, over)
    return out.reshape(bins, rows, width)


def solution(mesh):
    return jax.shard_map(
        shards,
        mesh=mesh,
        in_specs=(
            P("bins", "cells", None),
            P(None, "cells", None),
            P("cells", "bins"),
            P(),
            P(),
            P(),
            P(),
            P(),
        ),
        out_specs=P("bins", "cells", None),
        check_vma=False,
    )
```

```python
import functools

import jax
import jax.numpy as jnp
from jax import lax
from jax.experimental import pallas as pl
from jax.experimental.pallas import tpu as pltpu
from jax.sharding import PartitionSpec as P

STEP = 32
CHIPS = 4
ROWS = 8
INNER = [1, 2, 3, 4, 5, 6]
OUTER = [-1, 0, 1, 2, 5, 6, 7, 8]
LAST = [-1, 0, 1, 6, 7, 8]
KEPT = [1, 2, 5, 6]
PACK = 16
MIB = 2**20
SHRINK = 64


def shifted(value, axis, steps):
    count = lax.axis_size(axis)
    pairs = [(source, (source + steps) % count) for source in range(count)]
    return lax.ppermute(value, axis, pairs)


def swapped(value):
    return lax.ppermute(value, "bins", [(i, i ^ 1) for i in range(2 * CHIPS)])


def tied(value, *others):
    return lax.optimization_barrier((value, *others))[0]


def in_hbm(value):
    return pltpu.with_memory_space_constraint(value, pltpu.HBM)


def call(body, name, place, operands, outs, scratch, mib, flops, smem=0, far=(), out_far=False):
    vmem_spec = pl.BlockSpec(memory_space=pltpu.VMEM)
    smem_spec = pl.BlockSpec(memory_space=pltpu.SMEM)
    specs = [smem_spec] * (1 + smem) + [vmem_spec] * (len(operands) - smem)
    operands = list(operands)
    for index in far:
        specs[1 + index] = pl.BlockSpec(memory_space=pl.ANY)
        operands[index] = in_hbm(operands[index])
    moved = sum(a.size * a.dtype.itemsize for a in (*operands, *outs))
    return pl.pallas_call(
        body,
        in_specs=specs,
        out_specs=[pl.BlockSpec(memory_space=pl.ANY) if out_far else vmem_spec] * len(outs),
        out_shape=outs,
        scratch_shapes=scratch,
        compiler_params=pltpu.CompilerParams(vmem_limit_bytes=mib * MIB),
        cost_estimate=pl.CostEstimate(flops=flops // SHRINK, bytes_accessed=moved // SHRINK, transcendentals=0),
        name=name,
    )(place, *operands)


def steps(bins, body):
    def step(index, carry):
        body(pl.multiple_of(index * STEP, STEP))
        return carry

    lax.fori_loop(0, bins // STEP, step, 0)


def struct(shape, dtype):
    return jax.ShapeDtypeStruct(shape, dtype)


def rows_first(picked):
    shape = (len(picked) * STEP, STEP * ROWS)
    out = lax.broadcasted_iota(jnp.int32, shape, 0)
    inp = lax.broadcasted_iota(jnp.int32, shape, 1)
    slot, bin_of = out // STEP, out % STEP
    row = slot
    for index, value in enumerate(picked):
        row = jnp.where(slot == index, value, row)
    return jnp.where(inp == bin_of * ROWS + row, 1.0, 0.0).astype(jnp.bfloat16)


def bins_first():
    shape = (STEP * ROWS, ROWS * STEP)
    out = lax.broadcasted_iota(jnp.int32, shape, 0)
    inp = lax.broadcasted_iota(jnp.int32, shape, 1)
    return jnp.where(inp == (out % ROWS) * STEP + out // ROWS, 1.0, 0.0).astype(jnp.bfloat16)


def thirds(value):
    high = value.astype(jnp.bfloat16)
    rest = value - high.astype(jnp.float32)
    mid = rest.astype(jnp.bfloat16)
    low = (rest - mid.astype(jnp.float32)).astype(jnp.bfloat16)
    return [v.astype(jnp.float32) for v in (high, mid, low)]


def packed(rows):
    parts = [part for row in rows for part in thirds(row)]
    parts.append(jnp.zeros((PACK - len(parts), rows[0].shape[1]), jnp.float32))
    return jnp.concatenate(parts, 0).astype(jnp.bfloat16)


def unpacked(halo_ref, index):
    parts = halo_ref[0, halo_ref.shape[1] - PACK :, :].astype(jnp.float32)[3 * index : 3 * index + 3]
    return parts[0:1] + parts[1:2] + parts[2:3]


def edge_kernel(place_ref, source_ref, far_rate_ref, low_ref, high_ref, x_ref, rate_ref, onehot, sems, rate_sem):
    bins, width = low_ref.shape[1] - PACK, x_ref.shape[1]
    size = STEP * ROWS
    part_at = lambda index: pl.ds(index * size, size)
    copies = [
        pltpu.make_async_copy(source_ref.at[part_at(i)], x_ref.at[part_at(i)], sems.at[i]) for i in range(bins // STEP)
    ]
    rates_in = pltpu.make_async_copy(far_rate_ref, rate_ref, rate_sem)
    for copy in copies:
        copy.start()
    rates_in.start()
    onehot[...] = rows_first((0, 1, 6, 7))
    for index, copy in enumerate(copies):
        copy.wait()
        at = slice(index * STEP, (index + 1) * STEP)
        for lane in range(0, width, 256):
            lanes = slice(lane, lane + 256)
            part = jnp.dot(onehot[...], x_ref[part_at(index), lanes], preferred_element_type=jnp.float32)
            part = part.astype(jnp.bfloat16)
            for row in range(2):
                low_ref[row, at, lanes] = part[row * STEP : (row + 1) * STEP]
                high_ref[row, at, lanes] = part[(row + 2) * STEP : (row + 3) * STEP]
    rates_in.wait()
    low_ref[0, bins:, :] = packed([rate_ref[0, 0:1, :], rate_ref[1, 0:1, :]])
    high_ref[0, bins:, :] = packed([rate_ref[0, 6:7, :], rate_ref[0, 7:8, :], rate_ref[1, 7:8, :]])
    low_ref[1, bins:, :] = jnp.zeros((PACK, width), low_ref.dtype)
    high_ref[1, bins:, :] = jnp.zeros((PACK, width), low_ref.dtype)


def edge_rows(place, flat, courant):
    width, bins = flat.shape[1], flat.shape[0] // ROWS
    edge = struct((2, bins + PACK, width), flat.dtype)
    outs = [edge, edge, struct(flat.shape, flat.dtype), struct(courant.shape, courant.dtype)]
    scratch = [
        pltpu.VMEM((4 * STEP, STEP * ROWS), jnp.bfloat16),
        pltpu.SemaphoreType.DMA((bins // STEP,)),
        pltpu.SemaphoreType.DMA(()),
    ]
    return call(edge_kernel, "edge_rows", place, (flat, courant), outs, scratch, 4, 8 * STEP * flat.size, far=(0, 1))


def fill_coefs(coef, rates, rows):
    for index, row in enumerate(rows):
        face_x, face_y, under = rates(0, row), rates(1, row), rates(0, row - 1)
        face_x, face_y, under = (jnp.broadcast_to(v, (8, v.shape[1])) for v in (face_x, face_y, under))
        left = pltpu.roll(face_y, 1, 1)
        base = 5 * index
        own = 1.0 - jnp.maximum(face_x, 0.0) + jnp.minimum(under, 0.0)
        coef[base] = own - jnp.maximum(face_y, 0.0) + jnp.minimum(left, 0.0)
        coef[base + 1] = -jnp.minimum(face_x, 0.0)
        coef[base + 2] = jnp.maximum(under, 0.0)
        coef[base + 3] = -jnp.minimum(face_y, 0.0)
        coef[base + 4] = jnp.maximum(left, 0.0)


def substep(coef, index, before, value, after):
    width, base = value.shape[-1], 5 * index
    total = coef[base][None] * value + coef[base + 1][None] * after + coef[base + 2][None] * before
    total += coef[base + 3][None] * pltpu.roll(value, width - 1, 2)
    return total + coef[base + 4][None] * pltpu.roll(value, 1, 2)


def two_substeps(coef, held, load, rows, store, keep=lambda row, value: None):
    start, stop = rows[0], rows[-1]
    once = {}
    raw = {row: load(row) for row in (start - 2, start - 1)}
    for row in range(start - 1, stop + 2):
        raw[row + 1] = load(row + 1)
        once[row] = substep(coef, held.index(row), raw[row - 1], raw[row], raw[row + 1])
        keep(row, once[row])
        if row - 1 >= start:
            mid = row - 1
            store(mid, substep(coef, held.index(mid), once[mid - 1], once[mid], once[mid + 1]))


def grouped(value):
    return value.astype(jnp.float32).reshape(STEP // 8, 8, value.shape[-1])


def transpose_in(onehot, x_ref, field, start):
    width = x_ref.shape[1]
    source = pl.ds(pl.multiple_of(start * ROWS, STEP * ROWS), STEP * ROWS)
    for lane in range(0, width, 256):
        part = jnp.dot(onehot[...], x_ref[source, lane : lane + 256], preferred_element_type=jnp.float32)
        field[:, :, lane : lane + 256] = part.reshape(ROWS, STEP, 256)


def inner_kernel(place_ref, rate_ref, x_ref, out0, out1, out2, out3, coef, onehot, field, tiles):
    onehot[...] = rows_first(range(ROWS))
    fill_coefs(coef, lambda k, row: rate_ref[k, row : row + 1, :], INNER)

    def step(start):
        transpose_in(onehot, x_ref, field, start)
        load = lambda row: grouped(field[row])
        store = lambda row, value: send_row(place_ref, tiles, (out0, out1, out2, out3), row - 2, start, value)
        two_substeps(coef, INNER, load, range(2, 6), store)

    steps(out0.shape[2], step)


def send_row(place_ref, tiles, outs, slot, start, value):
    value = value.reshape(STEP, value.shape[-1]).astype(jnp.bfloat16)
    for tile in range(2 * CHIPS):
        tiles[tile] = value[:, tile * 128 : (tile + 1) * 128]
    for away, out_ref in enumerate(outs):
        chip = lax.rem(place_ref[0] + away, CHIPS)
        for core in range(2):
            out_ref[core, slot, pl.ds(start, STEP), :] = tiles[2 * chip + core]


def first_scratch(coefs, width, dtype):
    return [
        pltpu.VMEM((5 * coefs, 8, width), jnp.float32),
        pltpu.VMEM((ROWS * STEP, ROWS * STEP), jnp.bfloat16),
        pltpu.VMEM((ROWS, STEP, width), jnp.float32),
        pltpu.VMEM((2 * CHIPS, STEP, 128), dtype),
    ]


def inner_rows(place, courant, flat):
    width, bins = flat.shape[1], flat.shape[0] // ROWS
    outs = [struct((2, 4, bins, 128), flat.dtype)] * CHIPS
    scratch = first_scratch(len(INNER), width, flat.dtype)
    return call(inner_kernel, "inner_rows", place, (courant, flat), outs, scratch, 6, 120 * bins * width)


def all_rates(below_ref, rate_ref, above_ref):
    def rates(k, row):
        if row < 0:
            return unpacked(below_ref, row + 2 + k)
        if row > 7:
            return unpacked(above_ref, k)
        return rate_ref[k, row : row + 1, :]

    return rates


def outer_kernel(place_ref, rate_ref, under_ref, x_ref, over_ref, out0, out1, out2, out3, coef, onehot, field, tiles):
    onehot[...] = rows_first(range(ROWS))
    fill_coefs(coef, all_rates(under_ref, rate_ref, over_ref), OUTER)

    def step(start):
        transpose_in(onehot, x_ref, field, start)

        def load(row):
            if row < 0:
                return grouped(under_ref[row + 2, pl.ds(start, STEP), :])
            if row > 7:
                return grouped(over_ref[row - 8, pl.ds(start, STEP), :])
            return grouped(field[row])

        def store(row, value):
            send_row(place_ref, tiles, (out0, out1, out2, out3), row if row < 2 else row - 4, start, value)

        two_substeps(coef, OUTER, load, range(0, 2), store)
        two_substeps(coef, OUTER, load, range(6, 8), store)

    steps(out0.shape[2], step)


def outer_rows(place, courant, under, flat, over):
    width, bins = flat.shape[1], flat.shape[0] // ROWS
    outs = [struct((2, 4, bins, 128), flat.dtype)] * CHIPS
    scratch = first_scratch(len(OUTER), width, flat.dtype)
    operands = (courant, under, flat, over)
    return call(outer_kernel, "outer_rows", place, operands, outs, scratch, 6, 144 * bins * width)


def paired_kernel(place_ref, own_ref, *refs):
    for away in range(1, CHIPS):
        out_ref = refs[CHIPS - 2 + away]
        out_ref[0] = own_ref[away]
        out_ref[1] = refs[away - 1][...]


def paired_travel(place, own, *gives):
    got = [swapped(give) for give in gives]
    outs = [struct((2, *gives[0].shape), own.dtype)] * (CHIPS - 1)
    parts = call(paired_kernel, "paired", place, (own, *got[1:]), outs, [], 2, 0)
    return [own, got[0]] + [shifted(part, "bins", -2 * (away + 1)) for away, part in enumerate(parts)]


def arrived_kernel(place_ref, own_ref, got_ref, *refs):
    parts, (low_ref, high_ref) = refs[: CHIPS - 1], refs[CHIPS - 1 :]
    for away in range(CHIPS):
        for other in range(2):
            tile = 2 * lax.rem(place_ref[0] + away, CHIPS) + lax.bitwise_xor(place_ref[1], other)
            lanes = pl.ds(pl.multiple_of(tile * 128, 128), 128)
            slot = parts[away - 1].at[other] if away else got_ref if other else own_ref.at[0]
            for row in range(2):
                low_ref[row, :, lanes] = slot[row]
                high_ref[row, :, lanes] = slot[row + 2]


def arrived_rows(place, slots):
    _, bins, lanes = slots[1].shape
    outs = [struct((2, bins, 2 * CHIPS * lanes), slots[0].dtype)] * 2
    return call(arrived_kernel, "arrived_rows", place, slots, outs, [], 4, 0)


def middle_kernel(place_ref, rate_ref, low_ref, high_ref, *refs):
    slots, (mid_ref, kept_ref, coef, tiles) = refs[:8], refs[8:]
    core = place_ref[1]
    fill_coefs(coef, lambda k, row: rate_ref[k, row : row + 1, :], INNER)

    def step(start):
        at = pl.ds(start, STEP)
        for away in range(CHIPS):
            for other in range(2):
                tile = 2 * lax.rem(place_ref[0] + away, CHIPS) + lax.bitwise_xor(core, other)
                for row in range(4):
                    tiles[tile, row] = slots[2 * away + other][core, row, at, :]

        def load(row):
            if row < 2:
                return grouped(low_ref[row, at, :])
            if row > 5:
                return grouped(high_ref[row - 6, at, :])
            return grouped(jnp.concatenate([tiles[tile, row - 2] for tile in range(2 * CHIPS)], 1))

        def store(row, value):
            mid_ref[row - 2, at, :] = value.reshape(STEP, value.shape[-1]).astype(jnp.bfloat16)

        def keep(row, value):
            if row in KEPT:
                kept_ref[KEPT.index(row), at, :] = value.reshape(STEP, value.shape[-1])

        two_substeps(coef, INNER, load, range(2, 6), store, keep)

    steps(low_ref.shape[1], step)


def middle_rows(place, courant, low, high, slots):
    _, bins, width = low.shape
    outs = [struct((4, bins, width), low.dtype), struct((4, bins, width), jnp.float32)]
    scratch = [
        pltpu.VMEM((5 * len(INNER), 8, width), jnp.float32),
        pltpu.VMEM((2 * CHIPS, 4, STEP, 128), low.dtype),
    ]
    operands = (courant, low, high, *slots)
    return call(middle_kernel, "middle_rows", place, operands, outs, scratch, 5, 120 * bins * width)


def final_kernel(
    place_ref, first_under, rate_ref, first_over, under_ref, low_ref, mid_ref, kept_ref, high_ref, over_ref,
    far_ref, coef, onehot, back, out_ref, sems,
):
    width = out_ref.shape[1]
    onehot[...] = bins_first()
    fill_coefs(coef, all_rates(first_under, rate_ref, first_over), LAST)
    size = STEP * ROWS
    count = low_ref.shape[1] // STEP
    copies = []
    for index in range(count):
        at = slice(index * STEP, (index + 1) * STEP)
        field = lambda ref, row: grouped(ref[row, at, :])

        def store(row, value):
            back[row * STEP : (row + 1) * STEP, :] = value.reshape(STEP, width).astype(jnp.bfloat16)

        def once(row, before, value, after):
            return substep(coef, LAST.index(row), before, value, after)

        zero, one = field(low_ref, 0), field(kept_ref, 0)
        edge = once(-1, field(under_ref, 0), field(under_ref, 1), zero)
        first = once(0, field(under_ref, 1), zero, field(low_ref, 1))
        store(0, once(0, edge, first, one))
        store(1, once(1, first, one, field(kept_ref, 1)))
        seven, six = field(high_ref, 1), field(kept_ref, 3)
        edge = once(8, seven, field(over_ref, 0), field(over_ref, 1))
        last = once(7, field(high_ref, 0), seven, field(over_ref, 0))
        store(7, once(7, six, last, edge))
        store(6, once(6, field(kept_ref, 2), six, last))
        for row in range(4):
            back[(row + 2) * STEP : (row + 3) * STEP, :] = mid_ref[row, at, :]
        target = slice(index * size, (index + 1) * size)
        for lane in range(0, width, 256):
            part = jnp.dot(onehot[...], back[:, lane : lane + 256], preferred_element_type=jnp.float32)
            out_ref[target, lane : lane + 256] = part.astype(out_ref.dtype)
        copy = pltpu.make_async_copy(out_ref.at[pl.ds(index * size, size)], far_ref.at[pl.ds(index * size, size)], sems.at[index])
        copy.start()
        copies.append(copy)
    for copy in copies:
        copy.wait()


def final_rows(place, courant, first_under, first_over, under, low, mid, kept, high, over):
    _, bins, width = low.shape
    scratch = [
        pltpu.VMEM((5 * len(LAST), 8, width), jnp.float32),
        pltpu.VMEM((ROWS * STEP, ROWS * STEP), jnp.bfloat16),
        pltpu.VMEM((ROWS * STEP, width), low.dtype),
        pltpu.VMEM((bins * ROWS, width), low.dtype),
        pltpu.SemaphoreType.DMA((bins // STEP,)),
    ]
    operands = (first_under, courant, first_over, under, low, mid, kept, high, over)
    outs = [struct((bins * ROWS, width), low.dtype)]
    return call(final_kernel, "final_rows", place, operands, outs, scratch, 7, 96 * bins * width, out_far=True)[0]


def block_of(place_ref, away, other):
    return 2 * lax.rem(place_ref[0] + CHIPS - away, CHIPS) + lax.bitwise_xor(place_ref[1], other)


def matrices_kernel(
    place_ref, count_ref, far_pairs, growth_ref, far_kernel, far_redist, first_ref, second_ref, wide_ref,
    flags, pair_ref, kernel_ref, redist_ref, sems, pair_sem,
):
    nblocks, size = kernel_ref.shape[0], kernel_ref.shape[2]
    tile = place_ref[2]
    count = count_ref[tile]

    def copies(slot):
        row = block_of(place_ref, slot // 2, lax.rem(slot, 2))
        return [
            pltpu.make_async_copy(far.at[row], near.at[row], sems.at[side, slot])
            for side, (far, near) in enumerate(((far_kernel, kernel_ref), (far_redist, redist_ref)))
        ]

    pairs = pltpu.make_async_copy(far_pairs, pair_ref, pair_sem)
    pairs.start()
    for slot in range(nblocks):
        for copy in copies(slot):
            copy.start()
    pairs.wait()
    for index in range(nblocks * nblocks):
        flags[pair_ref[index, tile]] = jnp.where(index < count, 1, 0)
    blocks = [block_of(place_ref, away, other) for away in range(CHIPS) for other in range(2)]

    def row_step(slot, carry):
        row = block_of(place_ref, slot // 2, lax.rem(slot, 2))
        at = pl.ds(pl.multiple_of(slot * size, size), size)
        for copy in copies(slot):
            copy.wait()
        for index, col in enumerate(blocks):
            live = flags[row * nblocks + col] > 0
            lanes = slice(index * size, (index + 1) * size)
            for source, dest in ((kernel_ref, first_ref), (redist_ref, second_ref)):
                block = source[row, col]
                dest[at, lanes] = jnp.where(live, block, jnp.zeros_like(block))
        wide_ref[at, :] = jnp.broadcast_to(growth_ref[pl.ds(row, 1), :], (size, size)).T
        return carry

    lax.fori_loop(0, nblocks, row_step, 0)


def matrices(place, pair_lists, active_count, growth, kernel, redist):
    nblocks, size = kernel.shape[0], kernel.shape[2]
    bins = nblocks * size
    matrix = struct((bins, bins), kernel.dtype)
    outs = [matrix, matrix, struct((bins, size), jnp.float32)]
    operands = (active_count, pair_lists, growth, kernel, redist)
    scratch = [
        pltpu.SMEM((nblocks * nblocks,), jnp.int32),
        pltpu.SMEM(pair_lists.shape, jnp.int32),
        pltpu.VMEM(kernel.shape, kernel.dtype),
        pltpu.VMEM(redist.shape, redist.dtype),
        pltpu.SemaphoreType.DMA((2, nblocks)),
        pltpu.SemaphoreType.DMA(()),
    ]
    return call(matrices_kernel, "matrices", place, operands, outs, scratch, 6, 0, smem=1, far=(1, 3, 4))


def coagulate_kernel(picked, swap_first, place_ref, satur_ref, growth_ref, first_ref, second_ref, *refs):
    slots, outs, (field, losses, kept, moved) = refs[:8], refs[8:-4], refs[-4:]
    rows, size, lanes = slots[0].shape[1:]
    bins, cells = field.shape
    chip, core = place_ref[0], place_ref[1]
    half = bins // 2
    blocks = [block_of(place_ref, away, other) for away in range(CHIPS) for other in range(2)]
    for slot in range(2 * CHIPS):
        for r in range(rows):
            field[slot * size : (slot + 1) * size, r * lanes : (r + 1) * lanes] = slots[slot][core, r]
    for start in (0, half):
        at = slice(start, start + half)
        collide = jnp.dot(first_ref[at, :], field[...], preferred_element_type=jnp.float32)
        own = field[at, :].astype(jnp.float32)
        loss = own * collide
        losses[at, :] = loss.astype(jnp.bfloat16)
        kept[at, :] = own - loss
    satur = jnp.concatenate([satur_ref[r : r + 1, :] for r in picked], 1)
    for start in (0, half):
        at = slice(start, start + half)
        formed = jnp.dot(second_ref[at, :], losses[...], preferred_element_type=jnp.float32)
        after = kept[at, :] + formed
        growth = jnp.concatenate([growth_ref[at, :]] * rows, 1)
        flux = growth * satur * after
        kept[at, :] = after - flux
        moved[at, :] = flux
    for slot in range(2 * CHIPS):
        away, other = divmod(slot, 2)
        block = blocks[slot]
        below = lax.rem(block + 2 * CHIPS - 1, 2 * CHIPS)
        source = 2 * lax.rem(chip + CHIPS - below // 2, CHIPS) + lax.bitwise_xor(lax.rem(below, 2), core)
        last = moved[pl.ds(pl.multiple_of(source * size + size - 8, 8), 8), :][7:8, :]
        last = jnp.where(block > 0, last, jnp.zeros_like(last))
        at = slice(slot * size, (slot + 1) * size)
        inflow = pltpu.roll(moved[at, :], 1, 0)
        inflow = jnp.where(lax.broadcasted_iota(jnp.int32, inflow.shape, 0) == 0, last, inflow)
        middle = (kept[at, :] + inflow).astype(jnp.bfloat16)
        for r in range(rows):
            part = middle[:, r * lanes : (r + 1) * lanes]
            if not swap_first:
                outs[away][lax.bitwise_xor(core, other), r] = part
            elif other:
                outs[1 + away][r] = part
            else:
                outs[0][away, r] = part


def coagulate(picked, swap_first, place, satur, growth, first, second, slots):
    _, rows, size, lanes = slots[0].shape
    bins, cells = 2 * CHIPS * size, rows * lanes
    shape, dtype = slots[0].shape[1:], slots[0].dtype
    outs = [struct((2, *shape), dtype)] * CHIPS
    if swap_first:
        outs = [struct((CHIPS, *shape), dtype)] + [struct(shape, dtype)] * CHIPS
    scratch = [
        pltpu.VMEM((bins, cells), jnp.bfloat16),
        pltpu.VMEM((bins, cells), jnp.bfloat16),
        pltpu.VMEM((bins, cells), jnp.float32),
        pltpu.VMEM((bins, cells), jnp.float32),
    ]
    body = functools.partial(coagulate_kernel, picked, swap_first)
    operands = (satur, growth, first, second, *slots)
    return call(body, "coagulate", place, operands, outs, scratch, 10, 4 * bins * bins * cells)


def travel(parts, direction):
    return [parts[0]] + [shifted(parts[away], "bins", 2 * direction * away) for away in range(1, CHIPS)]


def with_other_core(parts):
    slots = []
    for part in parts:
        slots += [part, swapped(part)]
    return slots


def shards(concen, courant, saturation, growth, kernel, redist, pair_lists, active_count):
    bins, rows, width = concen.shape
    device = lax.axis_index("bins")
    tile_id = device * lax.axis_size("cells") + lax.axis_index("cells")
    place = jnp.stack([device // 2, device % 2, tile_id]).astype(jnp.int32)
    flat = concen.reshape(bins * rows, width)
    low, high, flat, courant = edge_rows(place, flat, courant)
    first_under, first_over = shifted(high, "cells", 1), shifted(low, "cells", -1)
    inner = inner_rows(place, courant, tied(flat, low))
    outer = outer_rows(place, courant, first_under, tied(flat, inner[0]), first_over)
    inner_slots = with_other_core([tied(part, outer[0]) for part in travel(inner, 1)])
    growth = growth.reshape(2 * CHIPS, bins)
    at = tied(place, *inner_slots[3::2])
    first, second, growth = matrices(at, pair_lists.T, active_count, growth, kernel, redist)
    inner = coagulate((2, 3, 4, 5), False, place, saturation, growth, first, second, inner_slots)
    outer_slots = with_other_core([tied(part, inner[0]) for part in travel(outer, 1)])
    outer = coagulate((0, 1, 6, 7), True, place, saturation, growth, first, second, outer_slots)

    outer_slots = paired_travel(place, *outer)
    inner_slots = with_other_core(travel([tied(part, outer[0]) for part in inner], -1))
    low, high = arrived_rows(place, outer_slots)
    under, over = shifted(high, "cells", 1), shifted(low, "cells", -1)
    mid, kept = middle_rows(place, courant, low, high, inner_slots)
    out = final_rows(place, courant, first_under, first_over, under, low, mid, kept, high, over)
    return out.reshape(bins, rows, width)


def solution(mesh):
    return jax.shard_map(
        shards,
        mesh=mesh,
        in_specs=(
            P("bins", "cells", None),
            P(None, "cells", None),
            P("cells", "bins"),
            P(),
            P(),
            P(),
            P(),
            P(),
        ),
        out_specs=P("bins", "cells", None),
        check_vma=False,
    )
```

```python
import functools

import jax
import jax.numpy as jnp
from jax import lax
from jax.experimental import pallas as pl
from jax.experimental.pallas import tpu as pltpu
from jax.sharding import PartitionSpec as P

STEP = 32
CHIPS = 4
ROWS = 8
INNER = [1, 2, 3, 4, 5, 6]
OUTER = [-1, 0, 1, 2, 5, 6, 7, 8]
LAST = [-1, 0, 1, 6, 7, 8]
KEPT = [1, 2, 5, 6]
PACK = 16
MIB = 2**20
SHRINK = 64


def shifted(value, axis, steps):
    count = lax.axis_size(axis)
    pairs = [(source, (source + steps) % count) for source in range(count)]
    return lax.ppermute(value, axis, pairs)


def swapped(value):
    return lax.ppermute(value, "bins", [(i, i ^ 1) for i in range(2 * CHIPS)])


def tied(value, *others):
    return lax.optimization_barrier((value, *others))[0]


def in_hbm(value):
    return pltpu.with_memory_space_constraint(value, pltpu.HBM)


def call(body, name, place, operands, outs, scratch, mib, flops, smem=0, far=(), out_far=False):
    vmem_spec = pl.BlockSpec(memory_space=pltpu.VMEM)
    smem_spec = pl.BlockSpec(memory_space=pltpu.SMEM)
    specs = [smem_spec] * (1 + smem) + [vmem_spec] * (len(operands) - smem)
    operands = list(operands)
    for index in far:
        specs[1 + index] = pl.BlockSpec(memory_space=pl.ANY)
        operands[index] = in_hbm(operands[index])
    moved = sum(a.size * a.dtype.itemsize for a in (*operands, *outs))
    return pl.pallas_call(
        body,
        in_specs=specs,
        out_specs=[pl.BlockSpec(memory_space=pl.ANY) if out_far else vmem_spec] * len(outs),
        out_shape=outs,
        scratch_shapes=scratch,
        compiler_params=pltpu.CompilerParams(vmem_limit_bytes=mib * MIB),
        cost_estimate=pl.CostEstimate(flops=flops // SHRINK, bytes_accessed=moved // SHRINK, transcendentals=0),
        name=name,
    )(place, *operands)


def steps(bins, body):
    def step(index, carry):
        body(pl.multiple_of(index * STEP, STEP))
        return carry

    lax.fori_loop(0, bins // STEP, step, 0)


def struct(shape, dtype):
    return jax.ShapeDtypeStruct(shape, dtype)


def rows_first(picked):
    shape = (len(picked) * STEP, STEP * ROWS)
    out = lax.broadcasted_iota(jnp.int32, shape, 0)
    inp = lax.broadcasted_iota(jnp.int32, shape, 1)
    slot, bin_of = out // STEP, out % STEP
    row = slot
    for index, value in enumerate(picked):
        row = jnp.where(slot == index, value, row)
    return jnp.where(inp == bin_of * ROWS + row, 1.0, 0.0).astype(jnp.bfloat16)


def bins_first():
    shape = (STEP * ROWS, ROWS * STEP)
    out = lax.broadcasted_iota(jnp.int32, shape, 0)
    inp = lax.broadcasted_iota(jnp.int32, shape, 1)
    return jnp.where(inp == (out % ROWS) * STEP + out // ROWS, 1.0, 0.0).astype(jnp.bfloat16)


def thirds(value):
    high = value.astype(jnp.bfloat16)
    rest = value - high.astype(jnp.float32)
    mid = rest.astype(jnp.bfloat16)
    low = (rest - mid.astype(jnp.float32)).astype(jnp.bfloat16)
    return [v.astype(jnp.float32) for v in (high, mid, low)]


def packed(rows):
    parts = [part for row in rows for part in thirds(row)]
    parts.append(jnp.zeros((PACK - len(parts), rows[0].shape[1]), jnp.float32))
    return jnp.concatenate(parts, 0).astype(jnp.bfloat16)


def unpacked(halo_ref, index):
    parts = halo_ref[0, halo_ref.shape[1] - PACK :, :].astype(jnp.float32)[3 * index : 3 * index + 3]
    return parts[0:1] + parts[1:2] + parts[2:3]


def edge_kernel(place_ref, source_ref, far_rate_ref, low_ref, high_ref, x_ref, rate_ref, onehot, sems, rate_sem):
    bins, width = low_ref.shape[1] - PACK, x_ref.shape[1]
    size = STEP * ROWS
    part_at = lambda index: pl.ds(index * size, size)
    copies = [
        pltpu.make_async_copy(source_ref.at[part_at(i)], x_ref.at[part_at(i)], sems.at[i]) for i in range(bins // STEP)
    ]
    rates_in = pltpu.make_async_copy(far_rate_ref, rate_ref, rate_sem)
    for copy in copies:
        copy.start()
    rates_in.start()
    onehot[...] = rows_first((0, 1, 6, 7))
    for index, copy in enumerate(copies):
        copy.wait()
        at = slice(index * STEP, (index + 1) * STEP)
        for lane in range(0, width, 256):
            lanes = slice(lane, lane + 256)
            part = jnp.dot(onehot[...], x_ref[part_at(index), lanes], preferred_element_type=jnp.float32)
            part = part.astype(jnp.bfloat16)
            for row in range(2):
                low_ref[row, at, lanes] = part[row * STEP : (row + 1) * STEP]
                high_ref[row, at, lanes] = part[(row + 2) * STEP : (row + 3) * STEP]
    rates_in.wait()
    low_ref[0, bins:, :] = packed([rate_ref[0, 0:1, :], rate_ref[1, 0:1, :]])
    high_ref[0, bins:, :] = packed([rate_ref[0, 6:7, :], rate_ref[0, 7:8, :], rate_ref[1, 7:8, :]])
    low_ref[1, bins:, :] = jnp.zeros((PACK, width), low_ref.dtype)
    high_ref[1, bins:, :] = jnp.zeros((PACK, width), low_ref.dtype)


def edge_rows(place, flat, courant):
    width, bins = flat.shape[1], flat.shape[0] // ROWS
    edge = struct((2, bins + PACK, width), flat.dtype)
    outs = [edge, edge, struct(flat.shape, flat.dtype), struct(courant.shape, courant.dtype)]
    scratch = [
        pltpu.VMEM((4 * STEP, STEP * ROWS), jnp.bfloat16),
        pltpu.SemaphoreType.DMA((bins // STEP,)),
        pltpu.SemaphoreType.DMA(()),
    ]
    return call(edge_kernel, "edge_rows", place, (flat, courant), outs, scratch, 4, 8 * STEP * flat.size, far=(0, 1))


def fill_coefs(coef, rates, rows):
    for index, row in enumerate(rows):
        face_x, face_y, under = rates(0, row), rates(1, row), rates(0, row - 1)
        face_x, face_y, under = (jnp.broadcast_to(v, (8, v.shape[1])) for v in (face_x, face_y, under))
        left = pltpu.roll(face_y, 1, 1)
        base = 5 * index
        own = 1.0 - jnp.maximum(face_x, 0.0) + jnp.minimum(under, 0.0)
        coef[base] = own - jnp.maximum(face_y, 0.0) + jnp.minimum(left, 0.0)
        coef[base + 1] = -jnp.minimum(face_x, 0.0)
        coef[base + 2] = jnp.maximum(under, 0.0)
        coef[base + 3] = -jnp.minimum(face_y, 0.0)
        coef[base + 4] = jnp.maximum(left, 0.0)


def substep(coef, index, before, value, after):
    width, base = value.shape[-1], 5 * index
    total = coef[base][None] * value + coef[base + 1][None] * after + coef[base + 2][None] * before
    total += coef[base + 3][None] * pltpu.roll(value, width - 1, 2)
    return total + coef[base + 4][None] * pltpu.roll(value, 1, 2)


def two_substeps(coef, held, load, rows, store, keep=lambda row, value: None):
    start, stop = rows[0], rows[-1]
    once = {}
    raw = {row: load(row) for row in (start - 2, start - 1)}
    for row in range(start - 1, stop + 2):
        raw[row + 1] = load(row + 1)
        once[row] = substep(coef, held.index(row), raw[row - 1], raw[row], raw[row + 1])
        keep(row, once[row])
        if row - 1 >= start:
            mid = row - 1
            store(mid, substep(coef, held.index(mid), once[mid - 1], once[mid], once[mid + 1]))


def grouped(value):
    return value.astype(jnp.float32).reshape(STEP // 8, 8, value.shape[-1])


def transpose_in(onehot, x_ref, field, start):
    width = x_ref.shape[1]
    source = pl.ds(pl.multiple_of(start * ROWS, STEP * ROWS), STEP * ROWS)
    for lane in range(0, width, 256):
        part = jnp.dot(onehot[...], x_ref[source, lane : lane + 256], preferred_element_type=jnp.float32)
        field[:, :, lane : lane + 256] = part.reshape(ROWS, STEP, 256)


def inner_kernel(place_ref, rate_ref, x_ref, own_ref, *refs):
    gives, (coef, onehot, field, tiles) = refs[:CHIPS], refs[CHIPS:]
    onehot[...] = rows_first(range(ROWS))
    fill_coefs(coef, lambda k, row: rate_ref[k, row : row + 1, :], INNER)

    def step(start):
        transpose_in(onehot, x_ref, field, start)
        load = lambda row: grouped(field[row])

        def store(row, value):
            value = value.reshape(STEP, value.shape[-1]).astype(jnp.bfloat16)
            for tile in range(2 * CHIPS):
                tiles[tile] = value[:, tile * 128 : (tile + 1) * 128]
            for away in range(CHIPS):
                chip, core = lax.rem(place_ref[0] + away, CHIPS), place_ref[1]
                own_ref[away, row - 2, pl.ds(start, STEP), :] = tiles[2 * chip + core]
                gives[away][row - 2, pl.ds(start, STEP), :] = tiles[2 * chip + 1 - core]

        two_substeps(coef, INNER, load, range(2, 6), store)

    steps(own_ref.shape[2], step)


def send_row(place_ref, tiles, outs, slot, start, value):
    value = value.reshape(STEP, value.shape[-1]).astype(jnp.bfloat16)
    for tile in range(2 * CHIPS):
        tiles[tile] = value[:, tile * 128 : (tile + 1) * 128]
    for away, out_ref in enumerate(outs):
        chip = lax.rem(place_ref[0] + away, CHIPS)
        for core in range(2):
            out_ref[core, slot, pl.ds(start, STEP), :] = tiles[2 * chip + core]


def first_scratch(coefs, width, dtype):
    return [
        pltpu.VMEM((5 * coefs, 8, width), jnp.float32),
        pltpu.VMEM((ROWS * STEP, ROWS * STEP), jnp.bfloat16),
        pltpu.VMEM((ROWS, STEP, width), jnp.float32),
        pltpu.VMEM((2 * CHIPS, STEP, 128), dtype),
    ]


def sides(shape, dtype):
    return [struct((CHIPS, *shape), dtype)] + [struct(shape, dtype)] * CHIPS


def inner_rows(place, courant, flat):
    width, bins = flat.shape[1], flat.shape[0] // ROWS
    outs = sides((4, bins, 128), flat.dtype)
    scratch = first_scratch(len(INNER), width, flat.dtype)
    return call(inner_kernel, "inner_rows", place, (courant, flat), outs, scratch, 6, 120 * bins * width)


def all_rates(below_ref, rate_ref, above_ref):
    def rates(k, row):
        if row < 0:
            return unpacked(below_ref, row + 2 + k)
        if row > 7:
            return unpacked(above_ref, k)
        return rate_ref[k, row : row + 1, :]

    return rates


def outer_kernel(place_ref, rate_ref, under_ref, x_ref, over_ref, out0, out1, out2, out3, coef, onehot, field, tiles):
    onehot[...] = rows_first(range(ROWS))
    fill_coefs(coef, all_rates(under_ref, rate_ref, over_ref), OUTER)

    def step(start):
        transpose_in(onehot, x_ref, field, start)

        def load(row):
            if row < 0:
                return grouped(under_ref[row + 2, pl.ds(start, STEP), :])
            if row > 7:
                return grouped(over_ref[row - 8, pl.ds(start, STEP), :])
            return grouped(field[row])

        def store(row, value):
            send_row(place_ref, tiles, (out0, out1, out2, out3), row if row < 2 else row - 4, start, value)

        two_substeps(coef, OUTER, load, range(0, 2), store)
        two_substeps(coef, OUTER, load, range(6, 8), store)

    steps(out0.shape[2], step)


def outer_rows(place, courant, under, flat, over):
    width, bins = flat.shape[1], flat.shape[0] // ROWS
    outs = [struct((2, 4, bins, 128), flat.dtype)] * CHIPS
    scratch = first_scratch(len(OUTER), width, flat.dtype)
    operands = (courant, under, flat, over)
    return call(outer_kernel, "outer_rows", place, operands, outs, scratch, 6, 144 * bins * width)


def paired_kernel(place_ref, own_ref, *refs):
    for away in range(1, CHIPS):
        out_ref = refs[CHIPS - 2 + away]
        out_ref[0] = own_ref[away]
        out_ref[1] = refs[away - 1][...]


def paired(place, own, *gives, early=False):
    got = [swapped(give) for give in gives]
    place = tied(place, got[0]) if early else place
    outs = [struct((2, *gives[0].shape), own.dtype)] * (CHIPS - 1)
    return own, got[0], call(paired_kernel, "paired", place, (own, *got[1:]), outs, [], 2, 0)


def spread(own, got, parts, direction):
    return [own, got] + [shifted(parts[away - 1], "bins", 2 * direction * away) for away in (2, 1, 3)]


def paired_slot(refs, away, other):
    return refs[(0, 3, 2, 4)[away]].at[other] if away else refs[1] if other else refs[0].at[0]


def arrived_kernel(place_ref, *refs):
    slots, (low_ref, high_ref) = refs[: CHIPS + 1], refs[CHIPS + 1 :]
    for away in range(CHIPS):
        for other in range(2):
            tile = 2 * lax.rem(place_ref[0] + away, CHIPS) + lax.bitwise_xor(place_ref[1], other)
            lanes = pl.ds(pl.multiple_of(tile * 128, 128), 128)
            slot = paired_slot(slots, away, other)
            for row in range(2):
                low_ref[row, :, lanes] = slot[row]
                high_ref[row, :, lanes] = slot[row + 2]


def arrived_rows(place, slots):
    _, bins, lanes = slots[1].shape
    outs = [struct((2, bins, 2 * CHIPS * lanes), slots[0].dtype)] * 2
    return call(arrived_kernel, "arrived_rows", place, slots, outs, [], 4, 0)


def middle_kernel(place_ref, rate_ref, low_ref, high_ref, *refs):
    slots, (mid_ref, kept_ref, coef, tiles) = refs[:8], refs[8:]
    core = place_ref[1]
    fill_coefs(coef, lambda k, row: rate_ref[k, row : row + 1, :], INNER)

    def step(start):
        at = pl.ds(start, STEP)
        for away in range(CHIPS):
            for other in range(2):
                tile = 2 * lax.rem(place_ref[0] + away, CHIPS) + lax.bitwise_xor(core, other)
                for row in range(4):
                    tiles[tile, row] = slots[2 * away + other][core, row, at, :]

        def load(row):
            if row < 2:
                return grouped(low_ref[row, at, :])
            if row > 5:
                return grouped(high_ref[row - 6, at, :])
            return grouped(jnp.concatenate([tiles[tile, row - 2] for tile in range(2 * CHIPS)], 1))

        def store(row, value):
            mid_ref[row - 2, at, :] = value.reshape(STEP, value.shape[-1]).astype(jnp.bfloat16)

        def keep(row, value):
            if row in KEPT:
                kept_ref[KEPT.index(row), at, :] = value.reshape(STEP, value.shape[-1])

        two_substeps(coef, INNER, load, range(2, 6), store, keep)

    steps(low_ref.shape[1], step)


def middle_rows(place, courant, low, high, slots):
    _, bins, width = low.shape
    outs = [struct((4, bins, width), low.dtype), struct((4, bins, width), jnp.float32)]
    scratch = [
        pltpu.VMEM((5 * len(INNER), 8, width), jnp.float32),
        pltpu.VMEM((2 * CHIPS, 4, STEP, 128), low.dtype),
    ]
    operands = (courant, low, high, *slots)
    return call(middle_kernel, "middle_rows", place, operands, outs, scratch, 5, 120 * bins * width)


def final_kernel(
    place_ref, first_under, rate_ref, first_over, under_ref, low_ref, mid_ref, kept_ref, high_ref, over_ref,
    far_ref, coef, onehot, back, out_ref, sems,
):
    width = out_ref.shape[1]
    onehot[...] = bins_first()
    fill_coefs(coef, all_rates(first_under, rate_ref, first_over), LAST)
    size = STEP * ROWS
    count = low_ref.shape[1] // STEP
    copies = []
    for index in range(count):
        at = slice(index * STEP, (index + 1) * STEP)
        field = lambda ref, row: grouped(ref[row, at, :])

        def store(row, value):
            back[row * STEP : (row + 1) * STEP, :] = value.reshape(STEP, width).astype(jnp.bfloat16)

        def once(row, before, value, after):
            return substep(coef, LAST.index(row), before, value, after)

        zero, one = field(low_ref, 0), field(kept_ref, 0)
        edge = once(-1, field(under_ref, 0), field(under_ref, 1), zero)
        first = once(0, field(under_ref, 1), zero, field(low_ref, 1))
        store(0, once(0, edge, first, one))
        store(1, once(1, first, one, field(kept_ref, 1)))
        seven, six = field(high_ref, 1), field(kept_ref, 3)
        edge = once(8, seven, field(over_ref, 0), field(over_ref, 1))
        last = once(7, field(high_ref, 0), seven, field(over_ref, 0))
        store(7, once(7, six, last, edge))
        store(6, once(6, field(kept_ref, 2), six, last))
        for row in range(4):
            back[(row + 2) * STEP : (row + 3) * STEP, :] = mid_ref[row, at, :]
        target = slice(index * size, (index + 1) * size)
        for lane in range(0, width, 256):
            part = jnp.dot(onehot[...], back[:, lane : lane + 256], preferred_element_type=jnp.float32)
            out_ref[target, lane : lane + 256] = part.astype(out_ref.dtype)
        copy = pltpu.make_async_copy(out_ref.at[pl.ds(index * size, size)], far_ref.at[pl.ds(index * size, size)], sems.at[index])
        copy.start()
        copies.append(copy)
    for copy in copies:
        copy.wait()


def final_rows(place, courant, first_under, first_over, under, low, mid, kept, high, over):
    _, bins, width = low.shape
    scratch = [
        pltpu.VMEM((5 * len(LAST), 8, width), jnp.float32),
        pltpu.VMEM((ROWS * STEP, ROWS * STEP), jnp.bfloat16),
        pltpu.VMEM((ROWS * STEP, width), low.dtype),
        pltpu.VMEM((bins * ROWS, width), low.dtype),
        pltpu.SemaphoreType.DMA((bins // STEP,)),
    ]
    operands = (first_under, courant, first_over, under, low, mid, kept, high, over)
    outs = [struct((bins * ROWS, width), low.dtype)]
    return call(final_kernel, "final_rows", place, operands, outs, scratch, 7, 96 * bins * width, out_far=True)[0]


def block_of(place_ref, away, other):
    return 2 * lax.rem(place_ref[0] + CHIPS - away, CHIPS) + lax.bitwise_xor(place_ref[1], other)


def matrices_kernel(
    place_ref, count_ref, far_pairs, growth_ref, far_kernel, far_redist, first_ref, second_ref, wide_ref,
    flags, pair_ref, kernel_ref, redist_ref, sems, pair_sem,
):
    nblocks, size = kernel_ref.shape[0], kernel_ref.shape[2]
    tile = place_ref[2]
    count = count_ref[tile]

    def copies(slot):
        row = block_of(place_ref, slot // 2, lax.rem(slot, 2))
        return [
            pltpu.make_async_copy(far.at[row], near.at[row], sems.at[side, slot])
            for side, (far, near) in enumerate(((far_kernel, kernel_ref), (far_redist, redist_ref)))
        ]

    pairs = pltpu.make_async_copy(far_pairs, pair_ref, pair_sem)
    pairs.start()
    for slot in range(nblocks):
        for copy in copies(slot):
            copy.start()
    pairs.wait()
    for index in range(nblocks * nblocks):
        flags[pair_ref[index, tile]] = jnp.where(index < count, 1, 0)
    blocks = [block_of(place_ref, away, other) for away in range(CHIPS) for other in range(2)]

    def row_step(slot, carry):
        row = block_of(place_ref, slot // 2, lax.rem(slot, 2))
        at = pl.ds(pl.multiple_of(slot * size, size), size)
        for copy in copies(slot):
            copy.wait()
        for index, col in enumerate(blocks):
            live = flags[row * nblocks + col] > 0
            lanes = slice(index * size, (index + 1) * size)
            for source, dest in ((kernel_ref, first_ref), (redist_ref, second_ref)):
                block = source[row, col]
                dest[at, lanes] = jnp.where(live, block, jnp.zeros_like(block))
        wide_ref[at, :] = jnp.broadcast_to(growth_ref[pl.ds(row, 1), :], (size, size)).T
        return carry

    lax.fori_loop(0, nblocks, row_step, 0)


def matrices(place, pair_lists, active_count, growth, kernel, redist):
    nblocks, size = kernel.shape[0], kernel.shape[2]
    bins = nblocks * size
    matrix = struct((bins, bins), kernel.dtype)
    outs = [matrix, matrix, struct((bins, size), jnp.float32)]
    operands = (active_count, pair_lists, growth, kernel, redist)
    scratch = [
        pltpu.SMEM((nblocks * nblocks,), jnp.int32),
        pltpu.SMEM(pair_lists.shape, jnp.int32),
        pltpu.VMEM(kernel.shape, kernel.dtype),
        pltpu.VMEM(redist.shape, redist.dtype),
        pltpu.SemaphoreType.DMA((2, nblocks)),
        pltpu.SemaphoreType.DMA(()),
    ]
    return call(matrices_kernel, "matrices", place, operands, outs, scratch, 6, 0, smem=1, far=(1, 3, 4))


def coagulate_kernel(picked, swap_first, place_ref, satur_ref, growth_ref, first_ref, second_ref, *refs):
    count = 2 * CHIPS if swap_first else CHIPS + 1
    slots, outs, (field, losses, kept, moved) = refs[:count], refs[count:-4], refs[-4:]
    rows, size, lanes = slots[1].shape[-3:]
    bins, cells = field.shape
    chip, core = place_ref[0], place_ref[1]
    half = bins // 2
    blocks = [block_of(place_ref, away, other) for away in range(CHIPS) for other in range(2)]
    for slot in range(2 * CHIPS):
        source = slots[slot].at[core] if swap_first else paired_slot(slots, *divmod(slot, 2))
        for r in range(rows):
            field[slot * size : (slot + 1) * size, r * lanes : (r + 1) * lanes] = source[r]
    for start in (0, half):
        at = slice(start, start + half)
        collide = jnp.dot(first_ref[at, :], field[...], preferred_element_type=jnp.float32)
        own = field[at, :].astype(jnp.float32)
        loss = own * collide
        losses[at, :] = loss.astype(jnp.bfloat16)
        kept[at, :] = own - loss
    satur = jnp.concatenate([satur_ref[r : r + 1, :] for r in picked], 1)
    for start in (0, half):
        at = slice(start, start + half)
        formed = jnp.dot(second_ref[at, :], losses[...], preferred_element_type=jnp.float32)
        after = kept[at, :] + formed
        growth = jnp.concatenate([growth_ref[at, :]] * rows, 1)
        flux = growth * satur * after
        kept[at, :] = after - flux
        moved[at, :] = flux
    for slot in range(2 * CHIPS):
        away, other = divmod(slot, 2)
        block = blocks[slot]
        below = lax.rem(block + 2 * CHIPS - 1, 2 * CHIPS)
        source = 2 * lax.rem(chip + CHIPS - below // 2, CHIPS) + lax.bitwise_xor(lax.rem(below, 2), core)
        last = moved[pl.ds(pl.multiple_of(source * size + size - 8, 8), 8), :][7:8, :]
        last = jnp.where(block > 0, last, jnp.zeros_like(last))
        at = slice(slot * size, (slot + 1) * size)
        inflow = pltpu.roll(moved[at, :], 1, 0)
        inflow = jnp.where(lax.broadcasted_iota(jnp.int32, inflow.shape, 0) == 0, last, inflow)
        middle = (kept[at, :] + inflow).astype(jnp.bfloat16)
        for r in range(rows):
            part = middle[:, r * lanes : (r + 1) * lanes]
            if not swap_first:
                outs[away][lax.bitwise_xor(core, other), r] = part
            elif other:
                outs[1 + away][r] = part
            else:
                outs[0][away, r] = part


def coagulate(picked, swap_first, place, satur, growth, first, second, slots):
    rows, size, lanes = slots[1].shape[-3:]
    bins, cells = 2 * CHIPS * size, rows * lanes
    shape, dtype = slots[1].shape[-3:], slots[1].dtype
    outs = [struct((2, *shape), dtype)] * CHIPS
    if swap_first:
        outs = sides(shape, dtype)
    scratch = [
        pltpu.VMEM((bins, cells), jnp.bfloat16),
        pltpu.VMEM((bins, cells), jnp.bfloat16),
        pltpu.VMEM((bins, cells), jnp.float32),
        pltpu.VMEM((bins, cells), jnp.float32),
    ]
    body = functools.partial(coagulate_kernel, picked, swap_first)
    operands = (satur, growth, first, second, *slots)
    return call(body, "coagulate", place, operands, outs, scratch, 10, 4 * bins * bins * cells)


def travel(parts, direction):
    sent = {away: shifted(parts[away], "bins", 2 * direction * away) for away in (1, 3, 2)}
    return [parts[0]] + [sent[away] for away in range(1, CHIPS)]


def with_other_core(parts):
    slots = []
    for part in parts:
        slots += [part, swapped(part)]
    return slots


def shards(concen, courant, saturation, growth, kernel, redist, pair_lists, active_count):
    bins, rows, width = concen.shape
    device = lax.axis_index("bins")
    tile_id = device * lax.axis_size("cells") + lax.axis_index("cells")
    place = jnp.stack([device // 2, device % 2, tile_id]).astype(jnp.int32)
    flat = concen.reshape(bins * rows, width)
    low, high, flat, courant = edge_rows(place, flat, courant)
    first_under, first_over = shifted(high, "cells", 1), shifted(low, "cells", -1)
    inner = paired(place, *inner_rows(place, courant, tied(flat, low)), early=True)
    outer = outer_rows(place, courant, first_under, tied(flat, inner[2][0]), first_over)
    inner = spread(*inner, 1)
    growth = growth.reshape(2 * CHIPS, bins)
    at = tied(place, outer[0])
    first, second, growth = matrices(at, pair_lists.T, active_count, growth, kernel, redist)
    inner = coagulate((2, 3, 4, 5), False, place, saturation, growth, first, second, inner)
    outer_slots = with_other_core([tied(part, inner[0]) for part in travel(outer, 1)])
    outer = coagulate((0, 1, 6, 7), True, place, saturation, growth, first, second, outer_slots)

    outer_slots = spread(*paired(place, *outer), -1)
    inner_slots = with_other_core(travel([tied(part, outer[0]) for part in inner], -1))
    low, high = arrived_rows(place, outer_slots)
    under, over = shifted(high, "cells", 1), shifted(low, "cells", -1)
    mid, kept = middle_rows(place, courant, low, high, inner_slots)
    out = final_rows(place, courant, first_under, first_over, under, low, mid, kept, high, over)
    return out.reshape(bins, rows, width)


def solution(mesh):
    return jax.shard_map(
        shards,
        mesh=mesh,
        in_specs=(
            P("bins", "cells", None),
            P(None, "cells", None),
            P("cells", "bins"),
            P(),
            P(),
            P(),
            P(),
            P(),
        ),
        out_specs=P("bins", "cells", None),
        check_vma=False,
    )
```

```python
import functools

import jax
import jax.numpy as jnp
from jax import lax
from jax.experimental import pallas as pl
from jax.experimental.pallas import tpu as pltpu
from jax.sharding import PartitionSpec as P

STEP = 32
CHIPS = 4
ROWS = 8
INNER = [1, 2, 3, 4, 5, 6]
LAST = [-1, 0, 1, 6, 7, 8]
KEPT = [1, 2, 5, 6]
LISTED = (0, 1, 3, 2)
PACK = 16
MIB = 2**20
SHRINK = 64


def shifted(value, axis, steps):
    count = lax.axis_size(axis)
    pairs = [(source, (source + steps) % count) for source in range(count)]
    return lax.ppermute(value, axis, pairs)


def swapped(value):
    return lax.ppermute(value, "bins", [(i, i ^ 1) for i in range(2 * CHIPS)])


def tied(value, *others):
    return lax.optimization_barrier((value, *others))[0]


def in_hbm(value):
    return pltpu.with_memory_space_constraint(value, pltpu.HBM)


def call(body, name, place, operands, outs, scratch, mib, flops, smem=0, far=(), out_far=False):
    vmem_spec = pl.BlockSpec(memory_space=pltpu.VMEM)
    smem_spec = pl.BlockSpec(memory_space=pltpu.SMEM)
    specs = [smem_spec] * (1 + smem) + [vmem_spec] * (len(operands) - smem)
    operands = list(operands)
    for index in far:
        specs[1 + index] = pl.BlockSpec(memory_space=pl.ANY)
        operands[index] = in_hbm(operands[index])
    moved = sum(a.size * a.dtype.itemsize for a in (*operands, *outs))
    near = [a for index, a in enumerate(operands) if index >= smem and index not in far] + ([] if out_far else list(outs))
    room = sum(a.size * a.dtype.itemsize for a in near) + mib * MIB
    return pl.pallas_call(
        body,
        in_specs=specs,
        out_specs=[pl.BlockSpec(memory_space=pl.ANY) if out_far else vmem_spec] * len(outs),
        out_shape=outs,
        scratch_shapes=scratch,
        compiler_params=pltpu.CompilerParams(vmem_limit_bytes=room),
        cost_estimate=pl.CostEstimate(flops=flops // SHRINK, bytes_accessed=moved // SHRINK, transcendentals=0),
        name=name,
    )(place, *operands)


def steps(bins, body):
    def step(index, carry):
        body(pl.multiple_of(index * STEP, STEP))
        return carry

    lax.fori_loop(0, bins // STEP, step, 0)


def struct(shape, dtype):
    return jax.ShapeDtypeStruct(shape, dtype)


def rows_first(picked):
    shape = (len(picked) * STEP, STEP * ROWS)
    out = lax.broadcasted_iota(jnp.int32, shape, 0)
    inp = lax.broadcasted_iota(jnp.int32, shape, 1)
    slot, bin_of = out // STEP, out % STEP
    row = slot
    for index, value in enumerate(picked):
        row = jnp.where(slot == index, value, row)
    return jnp.where(inp == bin_of * ROWS + row, 1.0, 0.0).astype(jnp.bfloat16)


def bins_first():
    shape = (STEP * ROWS, ROWS * STEP)
    out = lax.broadcasted_iota(jnp.int32, shape, 0)
    inp = lax.broadcasted_iota(jnp.int32, shape, 1)
    return jnp.where(inp == (out % ROWS) * STEP + out // ROWS, 1.0, 0.0).astype(jnp.bfloat16)


def thirds(value):
    high = value.astype(jnp.bfloat16)
    rest = value - high.astype(jnp.float32)
    mid = rest.astype(jnp.bfloat16)
    low = (rest - mid.astype(jnp.float32)).astype(jnp.bfloat16)
    return [v.astype(jnp.float32) for v in (high, mid, low)]


def packed(rows):
    parts = [part for row in rows for part in thirds(row)]
    parts.append(jnp.zeros((PACK - len(parts), rows[0].shape[1]), jnp.float32))
    return jnp.concatenate(parts, 0).astype(jnp.bfloat16)


def unpacked(halo_ref, index):
    parts = halo_ref[0, halo_ref.shape[1] - PACK :, :].astype(jnp.float32)[3 * index : 3 * index + 3]
    return parts[0:1] + parts[1:2] + parts[2:3]


def edge_kernel(place_ref, source_ref, far_rate_ref, low_ref, high_ref, x_ref, rate_ref, onehot, sems, rate_sem):
    bins, width = low_ref.shape[1] - PACK, x_ref.shape[1]
    size = STEP * ROWS
    part_at = lambda index: pl.ds(index * size, size)
    copies = [
        pltpu.make_async_copy(source_ref.at[part_at(i)], x_ref.at[part_at(i)], sems.at[i]) for i in range(bins // STEP)
    ]
    rates_in = pltpu.make_async_copy(far_rate_ref, rate_ref, rate_sem)
    for copy in copies:
        copy.start()
    rates_in.start()
    onehot[...] = rows_first((0, 1, 6, 7))
    for index, copy in enumerate(copies):
        copy.wait()
        at = slice(index * STEP, (index + 1) * STEP)
        for lane in range(0, width, 256):
            lanes = slice(lane, lane + 256)
            part = jnp.dot(onehot[...], x_ref[part_at(index), lanes], preferred_element_type=jnp.float32)
            part = part.astype(jnp.bfloat16)
            for row in range(2):
                low_ref[row, at, lanes] = part[row * STEP : (row + 1) * STEP]
                high_ref[row, at, lanes] = part[(row + 2) * STEP : (row + 3) * STEP]
    rates_in.wait()
    low_ref[0, bins:, :] = packed([rate_ref[0, 0:1, :], rate_ref[1, 0:1, :]])
    high_ref[0, bins:, :] = packed([rate_ref[0, 6:7, :], rate_ref[0, 7:8, :], rate_ref[1, 7:8, :]])
    low_ref[1, bins:, :] = jnp.zeros((PACK, width), low_ref.dtype)
    high_ref[1, bins:, :] = jnp.zeros((PACK, width), low_ref.dtype)


def edge_rows(place, flat, courant):
    width, bins = flat.shape[1], flat.shape[0] // ROWS
    edge = struct((2, bins + PACK, width), flat.dtype)
    outs = [edge, edge, struct(flat.shape, flat.dtype), struct(courant.shape, courant.dtype)]
    scratch = [
        pltpu.VMEM((4 * STEP, STEP * ROWS), jnp.bfloat16),
        pltpu.SemaphoreType.DMA((bins // STEP,)),
        pltpu.SemaphoreType.DMA(()),
    ]
    return call(edge_kernel, "edge_rows", place, (flat, courant), outs, scratch, 4, 8 * STEP * flat.size, far=(0, 1))


def fill_coefs(coef, rates, rows):
    for index, row in enumerate(rows):
        face_x, face_y, under = rates(0, row), rates(1, row), rates(0, row - 1)
        face_x, face_y, under = (jnp.broadcast_to(v, (8, v.shape[1])) for v in (face_x, face_y, under))
        left = pltpu.roll(face_y, 1, 1)
        base = 5 * index
        own = 1.0 - jnp.maximum(face_x, 0.0) + jnp.minimum(under, 0.0)
        coef[base] = own - jnp.maximum(face_y, 0.0) + jnp.minimum(left, 0.0)
        coef[base + 1] = -jnp.minimum(face_x, 0.0)
        coef[base + 2] = jnp.maximum(under, 0.0)
        coef[base + 3] = -jnp.minimum(face_y, 0.0)
        coef[base + 4] = jnp.maximum(left, 0.0)


def substep(coef, index, before, value, after):
    width, base = value.shape[-1], 5 * index
    total = coef[base][None] * value + coef[base + 1][None] * after + coef[base + 2][None] * before
    total += coef[base + 3][None] * pltpu.roll(value, width - 1, 2)
    return total + coef[base + 4][None] * pltpu.roll(value, 1, 2)


def two_substeps(coef, held, load, rows, store, keep=lambda row, value: None):
    start, stop = rows[0], rows[-1]
    once = {}
    raw = {row: load(row) for row in (start - 2, start - 1)}
    for row in range(start - 1, stop + 2):
        raw[row + 1] = load(row + 1)
        once[row] = substep(coef, held.index(row), raw[row - 1], raw[row], raw[row + 1])
        keep(row, once[row])
        if row - 1 >= start:
            mid = row - 1
            store(mid, substep(coef, held.index(mid), once[mid - 1], once[mid], once[mid + 1]))


def grouped(value):
    return value.astype(jnp.float32).reshape(STEP // 8, 8, value.shape[-1])


def transpose_in(onehot, x_ref, field, start):
    width = x_ref.shape[1]
    source = pl.ds(pl.multiple_of(start * ROWS, STEP * ROWS), STEP * ROWS)
    for lane in range(0, width, 256):
        part = jnp.dot(onehot[...], x_ref[source, lane : lane + 256], preferred_element_type=jnp.float32)
        field[:, :, lane : lane + 256] = part.reshape(ROWS, STEP, 256)


def inner_kernel(place_ref, rate_ref, x_ref, own_ref, *refs):
    gives, (kept_ref, coef, onehot, field, tiles) = refs[:CHIPS], refs[CHIPS:]
    onehot[...] = rows_first(range(ROWS))
    fill_coefs(coef, lambda k, row: rate_ref[k, row : row + 1, :], INNER)

    def step(start):
        transpose_in(onehot, x_ref, field, start)
        load = lambda row: grouped(field[row])

        def store(row, value):
            value = value.reshape(STEP, value.shape[-1]).astype(jnp.bfloat16)
            for tile in range(2 * CHIPS):
                tiles[tile] = value[:, tile * 128 : (tile + 1) * 128]
            for away in range(CHIPS):
                chip, core = lax.rem(place_ref[0] + away, CHIPS), place_ref[1]
                own_ref[away, row - 2, pl.ds(start, STEP), :] = tiles[2 * chip + core]
                gives[away][row - 2, pl.ds(start, STEP), :] = tiles[2 * chip + 1 - core]

        def keep(row, value):
            if row in KEPT:
                kept_ref[KEPT.index(row), pl.ds(start, STEP), :] = value.reshape(STEP, value.shape[-1])

        two_substeps(coef, INNER, load, range(2, 6), store, keep)

    steps(own_ref.shape[2], step)


def send_row(place_ref, tiles, outs, slot, start, value):
    value = value.reshape(STEP, value.shape[-1]).astype(jnp.bfloat16)
    for tile in range(2 * CHIPS):
        tiles[tile] = value[:, tile * 128 : (tile + 1) * 128]
    for away, out_ref in enumerate(outs):
        chip = lax.rem(place_ref[0] + away, CHIPS)
        for core in range(2):
            out_ref[core, slot, pl.ds(start, STEP), :] = tiles[2 * chip + core]


def first_scratch(coefs, width, dtype):
    return [
        pltpu.VMEM((5 * coefs, 8, width), jnp.float32),
        pltpu.VMEM((ROWS * STEP, ROWS * STEP), jnp.bfloat16),
        pltpu.VMEM((ROWS, STEP, width), jnp.float32),
        pltpu.VMEM((2 * CHIPS, STEP, 128), dtype),
    ]


def sides(shape, dtype):
    return [struct((CHIPS, *shape), dtype)] + [struct(shape, dtype)] * CHIPS


def inner_rows(place, courant, flat):
    width, bins = flat.shape[1], flat.shape[0] // ROWS
    outs = [*sides((4, bins, 128), flat.dtype), struct((4, bins, width), jnp.float32)]
    scratch = first_scratch(len(INNER), width, flat.dtype)
    return call(inner_kernel, "inner_rows", place, (courant, flat), outs, scratch, 6, 120 * bins * width)


def all_rates(below_ref, rate_ref, above_ref):
    def rates(k, row):
        if row < 0:
            return unpacked(below_ref, row + 2 + k)
        if row > 7:
            return unpacked(above_ref, k)
        return rate_ref[k, row : row + 1, :]

    return rates


def end_rows(coef, under_ref, low_ref, kept_ref, high_ref, over_ref, at, store):
    field = lambda ref, row: grouped(ref[row, at, :])

    def once(row, before, value, after):
        return substep(coef, LAST.index(row), before, value, after)

    zero, one = field(low_ref, 0), field(kept_ref, 0)
    edge = once(-1, field(under_ref, 0), field(under_ref, 1), zero)
    first = once(0, field(under_ref, 1), zero, field(low_ref, 1))
    store(0, once(0, edge, first, one))
    store(1, once(1, first, one, field(kept_ref, 1)))
    seven, six = field(high_ref, 1), field(kept_ref, 3)
    edge = once(8, seven, field(over_ref, 0), field(over_ref, 1))
    last = once(7, field(high_ref, 0), seven, field(over_ref, 0))
    store(7, once(7, six, last, edge))
    store(6, once(6, field(kept_ref, 2), six, last))


def outer_kernel(place_ref, rate_ref, under_ref, low_ref, kept_ref, high_ref, over_ref, out0, out1, out2, out3, coef, tiles):
    fill_coefs(coef, all_rates(under_ref, rate_ref, over_ref), LAST)

    def step(start):
        def store(row, value):
            value = value.reshape(STEP, value.shape[-1]).astype(jnp.bfloat16)
            for tile in range(2 * CHIPS):
                tiles[tile] = value[:, tile * 128 : (tile + 1) * 128]
            for away, out_ref in enumerate((out0, out1, out2, out3)):
                chip = lax.rem(place_ref[0] + away, CHIPS)
                for core in range(2):
                    out_ref[core, row if row < 2 else row - 4, pl.ds(start, STEP), :] = tiles[2 * chip + core]

        end_rows(coef, under_ref, low_ref, kept_ref, high_ref, over_ref, pl.ds(start, STEP), store)

    steps(out0.shape[2], step)


def outer_rows(place, courant, under, low, kept, high, over):
    _, bins, width = kept.shape
    outs = [struct((2, 4, bins, 128), low.dtype)] * CHIPS
    scratch = [pltpu.VMEM((5 * len(LAST), 8, width), jnp.float32), pltpu.VMEM((2 * CHIPS, STEP, 128), low.dtype)]
    operands = (courant, under, low, kept, high, over)
    return call(outer_kernel, "outer_rows", place, operands, outs, scratch, 6, 96 * bins * width)


def paired_kernel(place_ref, own_ref, *refs):
    for away in range(1, CHIPS):
        out_ref = refs[CHIPS - 2 + away]
        out_ref[0] = own_ref[away]
        out_ref[1] = refs[away - 1][...]


def paired(place, own, *gives, early=False):
    got = [swapped(give) for give in gives]
    place = tied(place, got[0]) if early else place
    outs = [struct((2, *gives[0].shape), own.dtype)] * (CHIPS - 1)
    return own, got[0], call(paired_kernel, "paired", place, (own, *got[1:]), outs, [], 2, 0)


def spread(own, got, parts, direction):
    return [own, got] + [shifted(parts[away - 1], "bins", 2 * direction * away) for away in (2, 1, 3)]


def paired_slot(refs, away, other):
    return refs[(0, 3, 2, 4)[away]].at[other] if away else refs[1] if other else refs[0].at[0]


def arrived_kernel(place_ref, *refs):
    slots, (low_ref, high_ref) = refs[: CHIPS + 1], refs[CHIPS + 1 :]
    for away in range(CHIPS):
        for other in range(2):
            tile = 2 * lax.rem(place_ref[0] + away, CHIPS) + lax.bitwise_xor(place_ref[1], other)
            lanes = pl.ds(pl.multiple_of(tile * 128, 128), 128)
            slot = paired_slot(slots, away, other)
            for row in range(2):
                low_ref[row, :, lanes] = slot[row]
                high_ref[row, :, lanes] = slot[row + 2]


def arrived_rows(place, slots):
    _, bins, lanes = slots[1].shape
    outs = [struct((2, bins, 2 * CHIPS * lanes), slots[0].dtype)] * 2
    return call(arrived_kernel, "arrived_rows", place, slots, outs, [], 4, 0)


def middle_kernel(place_ref, rate_ref, low_ref, high_ref, *refs):
    slots, (mid_ref, kept_ref, coef, tiles) = refs[:8], refs[8:]
    core = place_ref[1]
    fill_coefs(coef, lambda k, row: rate_ref[k, row : row + 1, :], INNER)

    def step(start):
        at = pl.ds(start, STEP)
        for away in range(CHIPS):
            for other in range(2):
                tile = 2 * lax.rem(place_ref[0] + away, CHIPS) + lax.bitwise_xor(core, other)
                for row in range(4):
                    tiles[tile, row] = slots[2 * away + other][core, row, at, :]

        def load(row):
            if row < 2:
                return grouped(low_ref[row, at, :])
            if row > 5:
                return grouped(high_ref[row - 6, at, :])
            return grouped(jnp.concatenate([tiles[tile, row - 2] for tile in range(2 * CHIPS)], 1))

        def store(row, value):
            mid_ref[row - 2, at, :] = value.reshape(STEP, value.shape[-1]).astype(jnp.bfloat16)

        def keep(row, value):
            if row in KEPT:
                kept_ref[KEPT.index(row), at, :] = value.reshape(STEP, value.shape[-1])

        two_substeps(coef, INNER, load, range(2, 6), store, keep)

    steps(low_ref.shape[1], step)


def middle_rows(place, courant, low, high, slots):
    _, bins, width = low.shape
    outs = [struct((4, bins, width), low.dtype), struct((4, bins, width), jnp.float32)]
    scratch = [
        pltpu.VMEM((5 * len(INNER), 8, width), jnp.float32),
        pltpu.VMEM((2 * CHIPS, 4, STEP, 128), low.dtype),
    ]
    operands = (courant, low, high, *slots)
    return call(middle_kernel, "middle_rows", place, operands, outs, scratch, 5, 120 * bins * width)


def final_kernel(
    place_ref, first_under, rate_ref, first_over, under_ref, low_ref, mid_ref, kept_ref, high_ref, over_ref,
    far_ref, coef, onehot, back, out_ref, sems,
):
    width = out_ref.shape[1]
    onehot[...] = bins_first()
    fill_coefs(coef, all_rates(first_under, rate_ref, first_over), LAST)
    size = STEP * ROWS
    count = low_ref.shape[1] // STEP
    copies = []
    for index in range(count):
        at = slice(index * STEP, (index + 1) * STEP)

        def store(row, value):
            back[index, row * STEP : (row + 1) * STEP, :] = value.reshape(STEP, width).astype(jnp.bfloat16)

        end_rows(coef, under_ref, low_ref, kept_ref, high_ref, over_ref, at, store)
        for row in range(4):
            back[index, (row + 2) * STEP : (row + 3) * STEP, :] = mid_ref[row, at, :]
        target = slice(index * size, (index + 1) * size)
        for lane in range(0, width, 256):
            part = jnp.dot(onehot[...], back[index, :, lane : lane + 256], preferred_element_type=jnp.float32)
            out_ref[target, lane : lane + 256] = part.astype(out_ref.dtype)
        copy = pltpu.make_async_copy(out_ref.at[pl.ds(index * size, size)], far_ref.at[pl.ds(index * size, size)], sems.at[index])
        copy.start()
        copies.append(copy)
    for copy in copies:
        copy.wait()


def final_rows(place, courant, first_under, first_over, under, low, mid, kept, high, over):
    _, bins, width = low.shape
    scratch = [
        pltpu.VMEM((5 * len(LAST), 8, width), jnp.float32),
        pltpu.VMEM((ROWS * STEP, ROWS * STEP), jnp.bfloat16),
        pltpu.VMEM((bins // STEP, ROWS * STEP, width), low.dtype),
        pltpu.VMEM((bins * ROWS, width), low.dtype),
        pltpu.SemaphoreType.DMA((bins // STEP,)),
    ]
    operands = (first_under, courant, first_over, under, low, mid, kept, high, over)
    outs = [struct((bins * ROWS, width), low.dtype)]
    return call(final_kernel, "final_rows", place, operands, outs, scratch, 10, 96 * bins * width, out_far=True)[0]


def block_of(place_ref, away, other):
    return 2 * lax.rem(place_ref[0] + CHIPS - away, CHIPS) + lax.bitwise_xor(place_ref[1], other)


def matrices_kernel(
    place_ref, count_ref, far_pairs, growth_ref, far_kernel, far_redist, first_ref, second_ref, wide_ref,
    flags, pair_ref, kernel_ref, redist_ref, sems, pair_sem,
):
    nblocks, size = kernel_ref.shape[0], kernel_ref.shape[2]
    tile = place_ref[2]
    count = count_ref[tile]

    def copies(slot):
        row = block_of(place_ref, slot // 2, lax.rem(slot, 2))
        return [
            pltpu.make_async_copy(far.at[row], near.at[row], sems.at[side, slot])
            for side, (far, near) in enumerate(((far_kernel, kernel_ref), (far_redist, redist_ref)))
        ]

    pairs = pltpu.make_async_copy(far_pairs, pair_ref, pair_sem)
    pairs.start()
    for slot in range(nblocks):
        for copy in copies(slot):
            copy.start()
    pairs.wait()
    for index in range(nblocks * nblocks):
        flags[pair_ref[index, tile]] = jnp.where(index < count, 1, 0)
    blocks = [block_of(place_ref, away, other) for away in range(CHIPS) for other in range(2)]

    def row_step(slot, carry):
        row = block_of(place_ref, slot // 2, lax.rem(slot, 2))
        at = pl.ds(pl.multiple_of(slot * size, size), size)
        for copy in copies(slot):
            copy.wait()
        for index, col in enumerate(blocks):
            live = flags[row * nblocks + col] > 0
            lanes = slice(index * size, (index + 1) * size)
            for source, dest in ((kernel_ref, first_ref), (redist_ref, second_ref)):
                block = source[row, col]
                dest[at, lanes] = jnp.where(live, block, jnp.zeros_like(block))
        wide_ref[at, :] = jnp.broadcast_to(growth_ref[pl.ds(row, 1), :], (size, size)).T
        return carry

    lax.fori_loop(0, nblocks, row_step, 0)


def matrices(place, pair_lists, active_count, growth, kernel, redist):
    nblocks, size = kernel.shape[0], kernel.shape[2]
    bins = nblocks * size
    matrix = struct((bins, bins), kernel.dtype)
    outs = [matrix, matrix, struct((bins, size), jnp.float32)]
    operands = (active_count, pair_lists, growth, kernel, redist)
    scratch = [
        pltpu.SMEM((nblocks * nblocks,), jnp.int32),
        pltpu.SMEM(pair_lists.shape, jnp.int32),
        pltpu.VMEM(kernel.shape, kernel.dtype),
        pltpu.VMEM(redist.shape, redist.dtype),
        pltpu.SemaphoreType.DMA((2, nblocks)),
        pltpu.SemaphoreType.DMA(()),
    ]
    return call(matrices_kernel, "matrices", place, operands, outs, scratch, 6, 0, smem=1, far=(1, 3, 4))


def coagulate_kernel(picked, swap_first, place_ref, satur_ref, growth_ref, first_ref, second_ref, *refs):
    count = 2 * CHIPS if swap_first else CHIPS + 1
    slots, outs, (field, losses, kept, moved) = refs[:count], refs[count:-4], refs[-4:]
    rows, size, lanes = slots[1].shape[-3:]
    bins, cells = field.shape
    chip, core = place_ref[0], place_ref[1]
    half = bins // 2
    blocks = [block_of(place_ref, away, other) for away in range(CHIPS) for other in range(2)]
    for slot in range(2 * CHIPS):
        away, other = divmod(slot, 2)
        if swap_first:
            source = slots[2 * LISTED.index(away) + other].at[core]
        else:
            source = paired_slot(slots, away, other)
        for r in range(rows):
            field[slot * size : (slot + 1) * size, r * lanes : (r + 1) * lanes] = source[r]
    for start in (0, half):
        at = slice(start, start + half)
        collide = jnp.dot(first_ref[at, :], field[...], preferred_element_type=jnp.float32)
        own = field[at, :].astype(jnp.float32)
        loss = own * collide
        losses[at, :] = loss.astype(jnp.bfloat16)
        kept[at, :] = own - loss
    satur = jnp.concatenate([satur_ref[r : r + 1, :] for r in picked], 1)
    for start in (0, half):
        at = slice(start, start + half)
        formed = jnp.dot(second_ref[at, :], losses[...], preferred_element_type=jnp.float32)
        after = kept[at, :] + formed
        growth = jnp.concatenate([growth_ref[at, :]] * rows, 1)
        flux = growth * satur * after
        kept[at, :] = after - flux
        moved[at, :] = flux
    for slot in range(2 * CHIPS):
        away, other = divmod(slot, 2)
        block = blocks[slot]
        below = lax.rem(block + 2 * CHIPS - 1, 2 * CHIPS)
        source = 2 * lax.rem(chip + CHIPS - below // 2, CHIPS) + lax.bitwise_xor(lax.rem(below, 2), core)
        last = moved[pl.ds(pl.multiple_of(source * size + size - 8, 8), 8), :][7:8, :]
        last = jnp.where(block > 0, last, jnp.zeros_like(last))
        at = slice(slot * size, (slot + 1) * size)
        inflow = pltpu.roll(moved[at, :], 1, 0)
        inflow = jnp.where(lax.broadcasted_iota(jnp.int32, inflow.shape, 0) == 0, last, inflow)
        middle = (kept[at, :] + inflow).astype(jnp.bfloat16)
        for r in range(rows):
            part = middle[:, r * lanes : (r + 1) * lanes]
            if not swap_first:
                outs[away][lax.bitwise_xor(core, other), r] = part
            elif other:
                outs[1 + away][r] = part
            else:
                outs[0][away, r] = part


def coagulate(picked, swap_first, place, satur, growth, first, second, slots):
    rows, size, lanes = slots[1].shape[-3:]
    bins, cells = 2 * CHIPS * size, rows * lanes
    shape, dtype = slots[1].shape[-3:], slots[1].dtype
    outs = [struct((2, *shape), dtype)] * CHIPS
    if swap_first:
        outs = sides(shape, dtype)
    scratch = [
        pltpu.VMEM((bins, cells), jnp.bfloat16),
        pltpu.VMEM((bins, cells), jnp.bfloat16),
        pltpu.VMEM((bins, cells), jnp.float32),
        pltpu.VMEM((bins, cells), jnp.float32),
    ]
    body = functools.partial(coagulate_kernel, picked, swap_first)
    operands = (satur, growth, first, second, *slots)
    return call(body, "coagulate", place, operands, outs, scratch, 10, 4 * bins * bins * cells)


def travel(parts, direction):
    sent = {away: shifted(parts[away], "bins", 2 * direction * away) for away in (1, 3, 2)}
    return [parts[0]] + [sent[away] for away in range(1, CHIPS)]


def with_other_core(parts, listed=range(CHIPS)):
    slots = []
    for away in listed:
        slots += [parts[away], swapped(parts[away])]
    return slots


def shards(concen, courant, saturation, growth, kernel, redist, pair_lists, active_count):
    bins, rows, width = concen.shape
    device = lax.axis_index("bins")
    tile_id = device * lax.axis_size("cells") + lax.axis_index("cells")
    place = jnp.stack([device // 2, device % 2, tile_id]).astype(jnp.int32)
    flat = concen.reshape(bins * rows, width)
    low, high, flat, courant = edge_rows(place, flat, courant)
    first_under, first_over = shifted(high, "cells", 1), shifted(low, "cells", -1)
    *inner, kept = inner_rows(place, courant, tied(flat, low))
    inner = paired(place, *inner, early=True)
    at = tied(place, inner[2][0])
    outer = outer_rows(at, courant, first_under, low, kept, high, first_over)
    inner = spread(*inner, 1)
    growth = growth.reshape(2 * CHIPS, bins)
    at = tied(place, outer[0])
    first, second, growth = matrices(at, pair_lists.T, active_count, growth, kernel, redist)
    inner = coagulate((2, 3, 4, 5), False, place, saturation, growth, first, second, inner)
    outer_slots = with_other_core([tied(part, inner[0]) for part in travel(outer, 1)], LISTED)
    outer = coagulate((0, 1, 6, 7), True, place, saturation, growth, first, second, outer_slots)

    outer_slots = spread(*paired(place, *outer), -1)
    inner_slots = with_other_core(travel([tied(part, outer[0]) for part in inner], -1))
    low, high = arrived_rows(place, outer_slots)
    under, over = shifted(high, "cells", 1), shifted(low, "cells", -1)
    mid, kept = middle_rows(place, courant, low, high, inner_slots)
    out = final_rows(place, courant, first_under, first_over, under, low, mid, kept, high, over)
    return out.reshape(bins, rows, width)


def solution(mesh):
    return jax.shard_map(
        shards,
        mesh=mesh,
        in_specs=(
            P("bins", "cells", None),
            P(None, "cells", None),
            P("cells", "bins"),
            P(),
            P(),
            P(),
            P(),
            P(),
        ),
        out_specs=P("bins", "cells", None),
        check_vma=False,
    )
```
